256 devices in a mesh: clu: 64 (over z, y, core), grp: 4 (over x).
Axes of the slice: x: 4, y: 4, z: 8, core: 2. Of those that a mesh axis runs over, the one named last changes fastest.
Arguments:
- embeddings: bfloat16 [131072, 768], P(('clu', 'grp')), may hold values from -6 to 6
- cluster_of: int32 [131072], P(('clu', 'grp')), may hold values from 0 to 127, as said below
- new_rows: bfloat16 [4096, 768], P(('clu', 'grp')), may hold values from -6 to 6
- centroids: bfloat16 [65536, 768], P(('clu', 'grp')), may hold values from -6 to 6
Outputs:
- dup_score: float32 [131072], P(('clu', 'grp'))
- centroid_score: float32 [4096], P(('clu', 'grp'))
The draws below stay inside these ranges and needn't reach their ends.
Inputs may be any that keep to these rules, and one draw needn't show every extreme that they name: `cluster_of`: cluster k is owned by owner k mod 64; among the 512 rows of one device, at most 16 rows belong to the clusters of one owner, and in every such block some owner has exactly 16.
All inputs are finite; a program needn't handle non-finite values.
Results may differ from the reference program's by a relative error of at most 0.0015.
Values may be sent and summed in bfloat16 or wider, within the bound.
No kernel may reach another device: no remote copies, remote signals or barrier semaphores. Data moves between devices by JAX's collectives and lax.ppermute only.
A program may use at most 64 MiB of HBM per device.

```python
import jax
import jax.numpy as jnp
from jax import lax

D = 768
TOK_DEV = 512
CPO = 2
CAP = 16
ROWS = 131072
NEW = 4096
CENT_DEV = 256
CENTROIDS = 65536
N_CLU = 64
N_GRP = 4


def draw_cluster_of(key, part):
    slot_cap = 2 * TOK_DEV // N_CLU
    slot_total = N_CLU * slot_cap

    def one_block(block_key):
        subkeys = jax.random.split(block_key, 4)
        forced = jax.random.randint(subkeys[0], (), 0, N_CLU)
        shuffled = jax.random.permutation(subkeys[1], slot_total)
        position = jnp.argsort(shuffled).astype(jnp.int32)
        slot_ids = jnp.arange(slot_total, dtype=jnp.int32)
        priority = jnp.where(slot_ids // slot_cap == forced, slot_ids - slot_total, position)
        chosen = jnp.argsort(priority)[:TOK_DEV].astype(jnp.int32)
        owner_ids = chosen // slot_cap
        within = jax.random.randint(subkeys[2], (TOK_DEV,), 0, CPO)
        clusters = owner_ids + N_CLU * within
        return jax.random.permutation(subkeys[3], clusters)
    block_keys = jax.vmap(lambda index_value: jax.random.fold_in(key, index_value))(jnp.arange(N_CLU * N_GRP))
    return jax.vmap(one_block)(block_keys).reshape(-1).astype(jnp.int32)


def shard_levels(own_key, shape, pieces, low, largest):
    def one(dim, shards_of):
        draws = jax.random.uniform(jax.random.fold_in(jax.random.fold_in(own_key, 6), dim), (shards_of,), jnp.float32, low / len(pieces), largest / len(pieces))
        return jnp.repeat(jnp.exp(draws), shape[dim] // shards_of).reshape((-1,) + (1,) * (len(shape) - dim - 1))

    gain = one(*pieces[0])
    for cut in pieces[1:]:
        gain = gain * one(*cut)
    return gain


def gaussian(stream_key, dims, width, most, pieces=(), kind=jnp.bfloat16):
    array = width * jax.random.normal(stream_key, dims, jnp.float32)
    if pieces:
        array = array * shard_levels(stream_key, dims, pieces, -0.22, 0.18)
    return jnp.clip(array, -most, most).astype(kind)


def setup_inputs(seed: int = 0) -> dict:
    key_list = jax.random.split(jax.random.key(seed), 5)
    return {
        "embeddings": gaussian(key_list[0], (ROWS, D), 1.0, 6.0, ((0, 256),)),
        "cluster_of": draw_cluster_of(jax.random.fold_in(key_list[4], 71), 0),
        "new_rows": gaussian(key_list[2], (NEW, D), 1.0, 6.0, ((0, 256),)),
        "centroids": gaussian(key_list[3], (CENTROIDS, D), 1.0, 6.0, ((0, 256),)),
    }


epsilon = 1e-06

def normalize(values):
    wide = values.astype(jnp.float32)
    total = lax.optimization_barrier(jnp.sum(wide * wide, axis=-1, keepdims=True))
    return (wide * lax.rsqrt(total + epsilon)).astype(jnp.bfloat16)

def reference(embeddings, cluster_of, new_rows, centroids):
    normed = normalize(embeddings)
    row_total = normed.shape[0]
    capacity = CAP * N_CLU * N_GRP
    owners = cluster_of % N_CLU
    ordering = jnp.argsort(owners, stable=True).astype(jnp.int32)
    per_owner = lax.optimization_barrier(jnp.sum((owners[None, :] == jnp.arange(N_CLU, dtype=jnp.int32)[:, None]).astype(jnp.int32), axis=1))
    offsets = (jnp.cumsum(per_owner) - per_owner).astype(jnp.int32)
    padded = jnp.concatenate([ordering, jnp.full((capacity,), row_total, jnp.int32)])
    diagonal = jnp.eye(capacity, dtype=bool)

    def one_owner(owner_idx):
        indices = lax.dynamic_slice(padded, (offsets[owner_idx],), (capacity,))
        is_valid = jnp.arange(capacity, dtype=jnp.int32) < per_owner[owner_idx]
        clamped = jnp.minimum(indices, row_total - 1)
        member_units = normed[clamped]
        member_cluster = jnp.where(is_valid, cluster_of[clamped], -1)
        scores = jnp.dot(member_units, member_units.T, preferred_element_type=jnp.float32)
        matched = (member_cluster[:, None] == member_cluster[None, :]) & is_valid[:, None] & jnp.logical_not(diagonal)
        best_match = lax.optimization_barrier(jnp.max(jnp.where(matched, scores, -1.0), axis=1))
        return (jnp.where(is_valid, indices, row_total), best_match)
    target_rows, maxima = lax.map(one_owner, jnp.arange(N_CLU, dtype=jnp.int32))
    dup_score = jnp.zeros((row_total + 1,), jnp.float32).at[target_rows.reshape(-1)].set(maxima.reshape(-1))[:row_total]
    new_unit = normalize(new_rows)
    cent_unit = normalize(centroids).reshape(-1, CENT_DEV, new_rows.shape[1])

    def absorb(running, block_units):
        scores = jnp.dot(new_unit, block_units.T, preferred_element_type=jnp.float32)
        return (jnp.maximum(running, lax.optimization_barrier(jnp.max(scores, axis=1))), None)
    start_value = jnp.full((new_unit.shape[0],), -jnp.inf, jnp.float32)
    centroid_score, unused = lax.scan(absorb, start_value, cent_unit)
    return (dup_score, centroid_score)
```

```python
import functools

import jax
import jax.numpy as jnp
from jax import lax
from jax.experimental import pallas as pl
from jax.experimental.pallas import tpu as pltpu
from jax.sharding import Mesh
from jax.sharding import PartitionSpec as P

EPS = 1e-06
OWN = ("z", "y", "xh")
ALL = ("z", "y", "c", "xh", "xl")
SWAP = [(0, 1), (1, 0)]
BF16 = jnp.bfloat16
F32 = jnp.float32
VMEM_LIMIT = 48 * 1024 * 1024


def unit_rows(rows):
    wide = rows.astype(F32)
    total = jnp.sum(wide * wide, axis=-1, keepdims=True)
    return (wide * lax.rsqrt(total + EPS)).astype(BF16)


def dot_t(left, right):
    return lax.dot_general(left, right, (((1,), (1,)), ((), ())), preferred_element_type=F32)


def params(**kwargs):
    return pltpu.CompilerParams(vmem_limit_bytes=VMEM_LIMIT, **kwargs)


def cost(flops, moved):
    return pl.CostEstimate(flops=flops, bytes_accessed=moved, transcendentals=0)


def column_to_grid(column, owners, cap):
    wide = jnp.broadcast_to(column.reshape(owners, cap, 1), (owners, cap, 128))
    sub = lax.broadcasted_iota(jnp.int32, (owners, cap, 128), 1)
    lane = lax.broadcasted_iota(jnp.int32, (owners, cap, 128), 2)
    return jnp.sum(jnp.where(sub == lane, wide, 0.0), axis=1)[:, :cap]


def pack_kernel(owners, cap, emb_ref, clu_ref, send_ref, ids_ref, place_ref):
    rows = emb_ref.shape[0]
    cluster = clu_ref[...]
    target = lax.rem(cluster, owners)
    owner_of = lax.broadcasted_iota(jnp.int32, (owners, rows), 0)
    hot = target == owner_of
    first = lax.broadcasted_iota(jnp.int32, (rows, rows), 0)
    second = lax.broadcasted_iota(jnp.int32, (rows, rows), 1)
    before = jnp.where(first < second, 1.0, 0.0).astype(BF16)
    ahead = jnp.dot(
        jnp.where(hot, 1.0, 0.0).astype(BF16), before, preferred_element_type=F32
    )
    rank = jnp.sum(jnp.where(hot, ahead, 0.0), axis=0, keepdims=True)
    rank_i = rank.astype(jnp.int32)
    slot = target * cap + rank_i
    place_ref[0:1, :] = target
    place_ref[1:2, :] = rank_i
    units = unit_rows(emb_ref[...])
    slots = owners * cap
    pick = jnp.where(
        lax.broadcasted_iota(jnp.int32, (slots, rows), 0) == slot, 1.0, 0.0
    ).astype(BF16)
    send_ref[...] = jnp.dot(pick, units, preferred_element_type=F32).astype(BF16)
    code = jnp.where(hot, cluster.astype(F32) + 1.0, 0.0)
    lane = lax.broadcasted_iota(jnp.int32, (owners, cap), 1)
    ids = jnp.full((owners, cap), -1.0, F32)
    for k in range(cap):
        held = jnp.sum(jnp.where(rank_i == k, code, 0.0), axis=1, keepdims=True)
        ids = jnp.where(lane == k, held - 1.0, ids)
    ids_ref[...] = ids.astype(BF16)


def pack(emb, cluster, owners, cap):
    rows, width = emb.shape
    return pl.pallas_call(
        functools.partial(pack_kernel, owners, cap),
        out_shape=(
            jax.ShapeDtypeStruct((owners * cap, width), BF16),
            jax.ShapeDtypeStruct((owners, cap), BF16),
            jax.ShapeDtypeStruct((2, rows), jnp.int32),
        ),
        compiler_params=params(),
        cost_estimate=cost(2 * owners * cap * rows * width, 3 * rows * width * 2),
    )(emb, cluster.reshape(1, rows))


def cent_kernel(owners, cap, new_ref, *refs):
    cent_refs, out_ref = refs[:-1], refs[-1]
    new_unit = unit_rows(new_ref[...])
    best = None
    for cent_ref in cent_refs:
        scores = dot_t(new_unit, unit_rows(cent_ref[...]))
        top = jnp.max(scores, axis=1, keepdims=True)
        best = top if best is None else jnp.maximum(best, top)
    out_ref[...] = column_to_grid(best, owners, cap)


def cent_best(new_all, cents, owners, cap):
    rows, width = new_all.shape
    count = sum(c.shape[0] for c in cents)
    return pl.pallas_call(
        functools.partial(cent_kernel, owners, cap),
        out_shape=jax.ShapeDtypeStruct((owners, cap), F32),
        compiler_params=params(),
        cost_estimate=cost(2 * rows * count * width, (rows + count) * width * 2),
    )(new_all, *cents)


def dup_kernel(with_self, tiles, own_ref, a_ref, b_ref, idc_ref, ida_ref, idb_ref, old_ref, out_ref, acc):
    step = pl.program_id(0)
    rows = own_ref.shape[0]
    tile = a_ref.shape[0]

    @pl.when(step == 0)
    def _():
        acc[...] = jnp.full(acc.shape, -1.0, F32)

    def fold(other_ref, ids_ref, diagonal):
        scores = dot_t(own_ref[...], other_ref[...])
        match = idc_ref[...] == ids_ref[...]
        if diagonal:
            row = lax.broadcasted_iota(jnp.int32, (rows, tile), 0)
            col = lax.broadcasted_iota(jnp.int32, (rows, tile), 1) + step * tile
            match = match & (row != col)
        kept = jnp.where(match, scores, -1.0)
        best = acc[...]
        for k in range(tile // 128):
            best = jnp.maximum(best, kept[:, k * 128 : (k + 1) * 128])
        acc[...] = best

    fold(a_ref, ida_ref, with_self)
    fold(b_ref, idb_ref, False)

    @pl.when(step == tiles - 1)
    def _():
        out_ref[...] = jnp.maximum(old_ref[...], jnp.max(acc[...], axis=1, keepdims=True))


def dup_best(own, a, b, idc, ida, idb, old, with_self):
    rows, width = own.shape
    tile = 256
    tiles = a.shape[0] // tile
    whole = lambda shape: pl.BlockSpec(shape, lambda j: (0, 0))
    return pl.pallas_call(
        functools.partial(dup_kernel, with_self, tiles),
        grid=(tiles,),
        in_specs=[
            whole((rows, width)),
            pl.BlockSpec((tile, width), lambda j: (j, 0)),
            pl.BlockSpec((tile, width), lambda j: (j, 0)),
            whole((rows, 1)),
            pl.BlockSpec((1, tile), lambda j: (0, j)),
            pl.BlockSpec((1, tile), lambda j: (0, j)),
            whole((rows, 1)),
        ],
        out_specs=whole((rows, 1)),
        out_shape=jax.ShapeDtypeStruct((rows, 1), F32),
        scratch_shapes=[pltpu.VMEM((rows, 128), F32)],
        compiler_params=params(),
        cost_estimate=cost(4 * rows * a.shape[0] * width, (rows + 2 * a.shape[0]) * width * 2),
    )(own, a, b, idc, ida, idb, old)


def unpack_kernel(owners, cap, back_ref, place_ref, dup_ref, cent_ref):
    back = back_ref[...]
    target = place_ref[0:1, :]
    rank = place_ref[1:2, :]
    rows = target.shape[1]
    found = jnp.full((owners, rows), -2.0, F32)
    for k in range(cap):
        found = jnp.where(rank == k, back[:, k : k + 1], found)
    owner_of = lax.broadcasted_iota(jnp.int32, (owners, rows), 0)
    dup_ref[...] = jnp.max(jnp.where(target == owner_of, found, -2.0), axis=0, keepdims=True)
    cent_ref[...] = jnp.max(back[:, cap:], axis=0, keepdims=True)


def unpack(back, place, owners, cap):
    rows = place.shape[1]
    return pl.pallas_call(
        functools.partial(unpack_kernel, owners, cap),
        out_shape=(
            jax.ShapeDtypeStruct((1, rows), F32),
            jax.ShapeDtypeStruct((1, back.shape[1] - cap), F32),
        ),
        compiler_params=params(),
    )(back, place)


def shards(embeddings, cluster_of, new_rows, centroids):
    owners = lax.axis_size(OWN)
    rows, width = embeddings.shape
    cap = 2 * rows // owners
    slots = owners * cap

    new_all = lax.all_gather(new_rows, OWN, axis=0, tiled=True)
    cent_x = lax.ppermute(centroids, "xl", SWAP)
    cent_c = lax.ppermute(centroids, "c", SWAP)
    cent_cx = lax.ppermute(cent_x, "c", SWAP)

    send, send_ids, place = pack(embeddings, cluster_of, owners, cap)
    ids = lax.all_to_all(send_ids, OWN, split_axis=0, concat_axis=0, tiled=True)
    own = lax.all_to_all(
        send.reshape(owners, cap, width), OWN, split_axis=0, concat_axis=0, tiled=True
    ).reshape(slots, width)
    id_row = ids.astype(F32).reshape(1, slots)
    id_x = lax.ppermute(ids, "xl", SWAP)
    id_c = lax.ppermute(ids, "c", SWAP)
    id_cx = lax.ppermute(id_x, "c", SWAP)

    def as_row(held):
        flat = held.astype(F32).reshape(1, slots)
        return jnp.where(flat < 0, -2.0, flat)

    idc = id_row.reshape(slots, 1)
    own_x = lax.ppermute(own, "xl", SWAP)
    own_c = lax.ppermute(own, "c", SWAP)
    own_cx = lax.ppermute(own_x, "c", SWAP)
    start = jnp.full((slots, 1), -1.0, F32)
    near = dup_best(own, own, own_c, idc, as_row(ids), as_row(id_c), start, True)
    best = dup_best(own, own_x, own_cx, idc, as_row(id_x), as_row(id_cx), near, False)
    cent = cent_best(new_all, (centroids, cent_c, cent_x, cent_cx), owners, new_rows.shape[0])
    both = jnp.concatenate([best.reshape(owners, cap), cent], axis=1)
    back = lax.all_to_all(both, OWN, split_axis=0, concat_axis=0, tiled=True)
    dup, cent_score = unpack(back, place, owners, cap)
    return (dup.reshape(rows), cent_score.reshape(new_rows.shape[0]))


def solution(mesh):
    sizes = mesh.devices.shape
    owners, group = sizes
    halves = owners // 2
    inner = Mesh(mesh.devices.reshape(halves // 4, 4, 2, group // 2, 2), ALL)
    return jax.shard_map(
        shards,
        mesh=inner,
        in_specs=(P(ALL, None), P(ALL), P(ALL, None), P(ALL, None)),
        out_specs=(P(ALL), P(ALL)),
        check_vma=False,
    )
```

```python
import functools

import jax
import jax.numpy as jnp
from jax import lax
from jax.experimental import pallas as pl
from jax.experimental.pallas import tpu as pltpu
from jax.sharding import Mesh
from jax.sharding import PartitionSpec as P

EPS = 1e-06
OWN = ("z", "y", "xh")
ALL = ("z", "y", "c", "xh", "xl")
SWAP = [(0, 1), (1, 0)]
BF16 = jnp.bfloat16
F32 = jnp.float32
NOTE = 8
VMEM_LIMIT = 48 * 1024 * 1024


def unit_rows(rows):
    wide = rows.astype(F32)
    total = jnp.sum(wide * wide, axis=-1, keepdims=True)
    return (wide * lax.rsqrt(total + EPS)).astype(BF16)


def dot_t(left, right):
    return lax.dot_general(left, right, (((1,), (1,)), ((), ())), preferred_element_type=F32)


def params(**kwargs):
    return pltpu.CompilerParams(vmem_limit_bytes=VMEM_LIMIT, **kwargs)


def cost(flops, moved):
    return pl.CostEstimate(flops=flops, bytes_accessed=moved, transcendentals=0)


def column_to_grid(column, owners, cap):
    wide = jnp.broadcast_to(column.reshape(owners, cap, 1), (owners, cap, 128))
    sub = lax.broadcasted_iota(jnp.int32, (owners, cap, 128), 1)
    lane = lax.broadcasted_iota(jnp.int32, (owners, cap, 128), 2)
    return jnp.sum(jnp.where(sub == lane, wide, 0.0), axis=1)[:, :cap]


def pack_kernel(cap, emb_ref, clu_ref, send_ref, place_ref):
    owners = send_ref.shape[0]
    rows, width = emb_ref.shape
    cluster = clu_ref[...]
    target = lax.rem(cluster, owners)
    owner_of = lax.broadcasted_iota(jnp.int32, (owners, rows), 0)
    hot = target == owner_of
    first = lax.broadcasted_iota(jnp.int32, (rows, rows), 0)
    second = lax.broadcasted_iota(jnp.int32, (rows, rows), 1)
    before = jnp.where(first < second, 1.0, 0.0).astype(BF16)
    ahead = jnp.dot(
        jnp.where(hot, 1.0, 0.0).astype(BF16), before, preferred_element_type=F32
    )
    rank = jnp.sum(jnp.where(hot, ahead, 0.0), axis=0, keepdims=True).astype(jnp.int32)
    place_ref[0:1, :] = target
    place_ref[1:2, :] = rank
    units = unit_rows(emb_ref[...])
    slot = target * cap + rank
    row_of = lax.broadcasted_iota(jnp.int32, (owners * cap, rows), 0)
    pick = jnp.where(row_of == slot, 1.0, 0.0).astype(BF16)
    send = jnp.dot(pick, units, preferred_element_type=F32).astype(BF16)
    for k in range(width // 128):
        piece = send[:, k * 128 : (k + 1) * 128].reshape(owners, cap, 128)
        send_ref[:, k * cap : (k + 1) * cap, :] = piece
    code = jnp.where(hot, cluster.astype(F32) + 1.0, 0.0)
    lane = lax.broadcasted_iota(jnp.int32, (owners, 128), 1)
    ids = jnp.full((owners, 128), -1.0, F32)
    for k in range(cap):
        held = jnp.sum(jnp.where(rank == k, code, 0.0), axis=1, keepdims=True)
        ids = jnp.where(lane == k, held - 1.0, ids)
    notes = jnp.broadcast_to(ids.reshape(owners, 1, 128), (owners, NOTE, 128))
    send_ref[:, width // 128 * cap :, :] = notes.astype(BF16)


def pack(emb, cluster, owners, cap):
    rows, width = emb.shape
    return pl.pallas_call(
        functools.partial(pack_kernel, cap),
        out_shape=(
            jax.ShapeDtypeStruct((owners, width // 128 * cap + NOTE, 128), BF16),
            jax.ShapeDtypeStruct((2, rows), jnp.int32),
        ),
        compiler_params=params(),
        cost_estimate=cost(2 * owners * cap * rows * width, 3 * rows * width * 2),
    )(emb, cluster.reshape(1, rows))


def tie(array, *others):
    return pl.pallas_call(
        lambda *refs: None,
        in_specs=[pl.BlockSpec(memory_space=pl.ANY)] * (1 + len(others)),
        out_specs=pl.BlockSpec(memory_space=pl.ANY),
        out_shape=jax.ShapeDtypeStruct(array.shape, array.dtype),
        input_output_aliases={0: 0},
    )(array, *others)


def cent_kernel(owners, cap, steps_y, steps_z, where_ref, mine_ref, other_ref, *refs):
    cent_refs, out_refs = refs[:-2], refs[-2:]
    at_z, at_y, at_xh = where_ref[0], where_ref[1], where_ref[2]
    units = [unit_rows(c[...]) for c in cent_refs]
    for new_ref, out_ref in zip((mine_ref, other_ref), out_refs):
        new_unit = unit_rows(new_ref[...])
        best = None
        for unit in units:
            top = jnp.max(dot_t(new_unit, unit), axis=1, keepdims=True)
            best = top if best is None else jnp.maximum(best, top)
        grid = column_to_grid(best, new_unit.shape[0] // cap, cap)
        out_ref[...] = jnp.full((owners, cap), -3.0, F32)
        k = 0
        for dy in steps_y:
            for dz in steps_z:
                source = lax.rem(at_z + dz, 8) * 4 + lax.rem(at_y + 4 + dy, 4)
                out_ref[pl.ds(source * 2 + at_xh, 1), :] = grid[k : k + 1, :]
                k += 1


def cent_best(where, mine, other, cents, owners, cap, steps_y, steps_z):
    rows, width = mine.shape
    count = sum(c.shape[0] for c in cents)
    vmem = pl.BlockSpec(memory_space=pltpu.VMEM)
    return pl.pallas_call(
        functools.partial(cent_kernel, owners, cap, steps_y, steps_z),
        in_specs=[pl.BlockSpec(memory_space=pltpu.SMEM)] + [vmem] * (2 + len(cents)),
        out_shape=(jax.ShapeDtypeStruct((owners, cap), F32),) * 2,
        compiler_params=params(),
        cost_estimate=cost(4 * rows * count * width, (2 * rows + count) * width * 2),
    )(where, mine, other, *cents)


def block_rows(block, cap):
    blocks, deep, _ = block.shape
    pieces = (deep - NOTE) // cap
    return jnp.concatenate(
        [block[:, k * cap : (k + 1) * cap, :].reshape(blocks * cap, 128) for k in range(pieces)],
        axis=1,
    )


def block_ids(block, cap):
    blocks, deep, _ = block.shape
    notes = block[:, deep - NOTE :, :].astype(F32)[:, 0:1, :]
    sub = lax.broadcasted_iota(jnp.int32, (blocks, cap, 128), 1)
    lane = lax.broadcasted_iota(jnp.int32, (blocks, cap, 128), 2)
    spread = jnp.where(sub == lane, jnp.broadcast_to(notes, (blocks, cap, 128)), 0.0)
    return spread.reshape(blocks * cap, 128)


def dup_kernel(tiles, cap, count, with_self, first, last, own_ref, *refs):
    col_refs, refs = refs[:count], refs[count:]
    if not first:
        old_ref, refs = refs[0], refs[1:]
    if last:
        cent_refs, refs = refs[:2], refs[2:]
    out_ref, own, own_ids = refs[:3]
    acc = refs[3] if last else out_ref
    step = pl.program_id(0)
    rows = own.shape[0]

    @pl.when(step == 0)
    def _():
        acc[...] = jnp.full(acc.shape, -1.0, F32) if first else old_ref[...]
        own[...] = block_rows(own_ref[...], cap)
        own_ids[...] = jnp.sum(block_ids(own_ref[...], cap), axis=1, keepdims=True)

    for k, col_ref in enumerate(col_refs):
        block = col_ref[...]
        other = block_rows(block, cap)
        tile = other.shape[0]
        spread = block_ids(block, cap).astype(BF16)
        col_ids = dot_t(jnp.full((8, 128), 1.0, BF16), spread)[0:1, :]
        match = own_ids[...] == jnp.where(col_ids < 0, -2.0, col_ids)
        if with_self and k == 0:
            row = lax.broadcasted_iota(jnp.int32, (rows, tile), 0)
            col = lax.broadcasted_iota(jnp.int32, (rows, tile), 1) + step * tile
            match = match & (row != col)
        kept = jnp.where(match, dot_t(own[...], other), -1.0)
        best = acc[...]
        for j in range(tile // 128):
            best = jnp.maximum(best, kept[:, j * 128 : (j + 1) * 128])
        acc[...] = best

    if last:

        @pl.when(step == tiles - 1)
        def _():
            top = jnp.max(acc[...], axis=1, keepdims=True)
            out_ref[:, :cap] = column_to_grid(top, own_ref.shape[0], cap)
            out_ref[:, cap:] = jnp.maximum(cent_refs[0][...], cent_refs[1][...])


def dup_best(own, cols, cap, with_self=False, old=None, cents=None):
    owners, deep, _ = own.shape
    rows, width = owners * cap, (deep - NOTE) // cap * 128
    each = 16
    tiles = owners // each
    last = cents is not None
    whole = lambda array: pl.BlockSpec(array.shape, lambda j: (0,) * len(array.shape))
    held = jax.ShapeDtypeStruct((rows, 128), F32)
    out_shape = jax.ShapeDtypeStruct((owners, 2 * cap), F32) if last else held
    more = ([] if old is None else [old]) + (list(cents) if last else [])
    return pl.pallas_call(
        functools.partial(dup_kernel, tiles, cap, len(cols), with_self, old is None, last),
        grid=(tiles,),
        in_specs=[whole(own)]
        + [pl.BlockSpec((each, deep, 128), lambda j: (j, 0, 0))] * len(cols)
        + [whole(a) for a in more],
        out_specs=whole(out_shape),
        out_shape=out_shape,
        scratch_shapes=[pltpu.VMEM((rows, width), BF16), pltpu.VMEM((rows, 1), F32)]
        + ([pltpu.VMEM((rows, 128), F32)] if last else []),
        compiler_params=params(),
        cost_estimate=cost(
            2 * rows * rows * len(cols) * width, (1 + len(cols)) * rows * width * 2
        ),
    )(own, *cols, *more)


def unpack_kernel(owners, cap, back_ref, place_ref, dup_ref, cent_ref):
    back = back_ref[...]
    target = place_ref[0:1, :]
    rank = place_ref[1:2, :]
    rows = target.shape[1]
    found = jnp.full((owners, rows), -2.0, F32)
    for k in range(cap):
        found = jnp.where(rank == k, back[:, k : k + 1], found)
    owner_of = lax.broadcasted_iota(jnp.int32, (owners, rows), 0)
    dup_ref[...] = jnp.max(jnp.where(target == owner_of, found, -2.0), axis=0, keepdims=True)
    cent_ref[...] = jnp.max(back[:, cap:], axis=0, keepdims=True)


def unpack(back, place, owners, cap):
    rows = place.shape[1]
    return pl.pallas_call(
        functools.partial(unpack_kernel, owners, cap),
        out_shape=(
            jax.ShapeDtypeStruct((1, rows), F32),
            jax.ShapeDtypeStruct((1, back.shape[1] - cap), F32),
        ),
        compiler_params=params(),
    )(back, place)


def join_kernel(*refs):
    out_ref, at = refs[-1], 0
    for ref in refs[:-1]:
        out_ref[at : at + ref.shape[0], :] = ref[...]
        at += ref.shape[0]


def join(*blocks):
    rows, width = sum(b.shape[0] for b in blocks), blocks[0].shape[1]
    return pl.pallas_call(
        join_kernel,
        out_shape=jax.ShapeDtypeStruct((rows, width), blocks[0].dtype),
        compiler_params=params(),
        cost_estimate=cost(0, 4 * rows * width),
    )(*blocks)


def shards(embeddings, cluster_of, new_rows, centroids):
    owners = lax.axis_size(OWN)
    rows, width = embeddings.shape
    cap = 2 * rows // owners

    cents = lax.all_gather(centroids, ("xh", "xl"), axis=0, tiled=True)
    steps_z = tuple(range(8))
    line = [new_rows] + [
        lax.ppermute(new_rows, "z", [(i, (i + 8 - k) % 8) for i in range(8)]) for k in steps_z[1:]
    ]
    send, place = pack(embeddings, cluster_of, owners, cap)
    landed = lax.all_to_all(send, OWN, split_axis=0, concat_axis=0, tiled=True)
    line = join(*line)
    own = tie(landed, cents, line)

    own_x = lax.ppermute(own, "xl", SWAP)
    own_c = lax.ppermute(own, "c", SWAP)
    held = dup_best(own, [own, own_c], cap, with_self=True)

    steps_y = (0, -1, 1, -2)
    line = tie(line, own)
    left = lax.ppermute(line, "y", [(i, (i + 1) % 4) for i in range(4)])
    right = lax.ppermute(line, "y", [(i, (i + 3) % 4) for i in range(4)])
    far = lax.ppermute(left, "y", [(i, (i + 1) % 4) for i in range(4)])
    new = join(line, left, right, far)
    new_other = lax.ppermute(new, "c", SWAP)
    where = jnp.stack([lax.axis_index(a) for a in OWN]).astype(jnp.int32)
    cent_mine, cent_theirs = cent_best(
        where, new, new_other, (cents,), owners, new_rows.shape[0], steps_y, steps_z
    )
    cent_back = lax.ppermute(cent_theirs, "c", SWAP)

    own_cx = lax.ppermute(tie(own_x, held, cent_mine), "c", SWAP)
    held = dup_best(own, [own_x], cap, old=held)
    both = dup_best(own, [own_cx], cap, old=held, cents=[cent_mine, cent_back])
    back = lax.all_to_all(both, OWN, split_axis=0, concat_axis=0, tiled=True)
    dup, cent_score = unpack(back, place, owners, cap)
    return (dup.reshape(rows), cent_score.reshape(new_rows.shape[0]))


def solution(mesh):
    sizes = mesh.devices.shape
    owners, group = sizes
    halves = owners // 2
    inner = Mesh(mesh.devices.reshape(halves // 4, 4, 2, group // 2, 2), ALL)
    return jax.shard_map(
        shards,
        mesh=inner,
        in_specs=(P(ALL, None), P(ALL), P(ALL, None), P(ALL, None)),
        out_specs=(P(ALL), P(ALL)),
        check_vma=False,
    )
```

```python
import functools

import jax
import jax.numpy as jnp
from jax import lax
from jax.experimental import pallas as pl
from jax.experimental.pallas import tpu as pltpu
from jax.sharding import Mesh
from jax.sharding import PartitionSpec as P

EPS = 1e-06
OWN = ("z", "y", "xh")
ALL = ("z", "y", "c", "xh", "xl")
SWAP = [(0, 1), (1, 0)]
BF16 = jnp.bfloat16
F32 = jnp.float32
NOTE = 8
INFO = 16
VMEM_LIMIT = 48 * 1024 * 1024


def unit_rows(rows):
    wide = rows.astype(F32)
    total = jnp.sum(wide * wide, axis=-1, keepdims=True)
    return (wide * lax.rsqrt(total + EPS)).astype(BF16)


def dot_t(left, right):
    return lax.dot_general(left, right, (((1,), (1,)), ((), ())), preferred_element_type=F32)


def params(**kwargs):
    return pltpu.CompilerParams(vmem_limit_bytes=VMEM_LIMIT, **kwargs)


def cost(flops, moved):
    return pl.CostEstimate(flops=flops, bytes_accessed=moved, transcendentals=0)


def column_to_grid(column, owners, cap):
    wide = jnp.broadcast_to(column.reshape(owners, cap, 1), (owners, cap, 128))
    sub = lax.broadcasted_iota(jnp.int32, (owners, cap, 128), 1)
    lane = lax.broadcasted_iota(jnp.int32, (owners, cap, 128), 2)
    return jnp.sum(jnp.where(sub == lane, wide, 0.0), axis=1)[:, :cap]


def pack_kernel(cap, emb_ref, clu_ref, send_ref, place_ref):
    owners = send_ref.shape[0]
    rows, width = emb_ref.shape
    cluster = clu_ref[...]
    target = lax.rem(cluster, owners)
    owner_of = lax.broadcasted_iota(jnp.int32, (owners, rows), 0)
    hot = target == owner_of
    first = lax.broadcasted_iota(jnp.int32, (rows, rows), 0)
    second = lax.broadcasted_iota(jnp.int32, (rows, rows), 1)
    before = jnp.where(first < second, 1.0, 0.0).astype(BF16)
    ahead = jnp.dot(
        jnp.where(hot, 1.0, 0.0).astype(BF16), before, preferred_element_type=F32
    )
    rank = jnp.sum(jnp.where(hot, ahead, 0.0), axis=0, keepdims=True).astype(jnp.int32)
    place_ref[0:1, :] = target
    place_ref[1:2, :] = rank
    units = unit_rows(emb_ref[...])
    slot = target * cap + rank
    row_of = lax.broadcasted_iota(jnp.int32, (owners * cap, rows), 0)
    pick = jnp.where(row_of == slot, 1.0, 0.0).astype(BF16)
    send = jnp.dot(pick, units, preferred_element_type=F32).astype(BF16)
    for k in range(width // 128):
        piece = send[:, k * 128 : (k + 1) * 128].reshape(owners, cap, 128)
        send_ref[:, k * cap : (k + 1) * cap, :] = piece
    code = jnp.where(hot, cluster.astype(F32) + 1.0, 0.0)
    lane = lax.broadcasted_iota(jnp.int32, (owners, 128), 1)
    ids = jnp.full((owners, 128), -1.0, F32)
    for k in range(cap):
        held = jnp.sum(jnp.where(rank == k, code, 0.0), axis=1, keepdims=True)
        ids = jnp.where(lane == k, held - 1.0, ids)
    notes = jnp.broadcast_to(ids.reshape(owners, 1, 128), (owners, NOTE, 128))
    send_ref[:, width // 128 * cap :, :] = notes.astype(BF16)


def pack(emb, cluster, owners, cap):
    rows, width = emb.shape
    return pl.pallas_call(
        functools.partial(pack_kernel, cap),
        out_shape=(
            jax.ShapeDtypeStruct((owners, width // 128 * cap + NOTE, 128), BF16),
            jax.ShapeDtypeStruct((2, rows), jnp.int32),
        ),
        compiler_params=params(),
        cost_estimate=cost(2 * owners * cap * rows * width, 3 * rows * width * 2),
    )(emb, cluster.reshape(1, rows))


def tie(array, *others):
    return pl.pallas_call(
        lambda *refs: None,
        in_specs=[pl.BlockSpec(memory_space=pl.ANY)] * (1 + len(others)),
        out_specs=pl.BlockSpec(memory_space=pl.ANY),
        out_shape=jax.ShapeDtypeStruct(array.shape, array.dtype),
        input_output_aliases={0: 0},
    )(array, *others)


def cent_kernel(owners, cap, steps_y, steps_z, where_ref, mine_ref, other_ref, *refs):
    cent_refs, out_refs = refs[:-2], refs[-2:]
    at_z, at_y, at_xh = where_ref[0], where_ref[1], where_ref[2]
    units = [unit_rows(c[...]) for c in cent_refs]
    for new_ref, out_ref in zip((mine_ref, other_ref), out_refs):
        new_unit = unit_rows(new_ref[...])
        best = None
        for unit in units:
            top = jnp.max(dot_t(new_unit, unit), axis=1, keepdims=True)
            best = top if best is None else jnp.maximum(best, top)
        grid = column_to_grid(best, new_unit.shape[0] // cap, cap)
        out_ref[...] = jnp.full((owners, cap), -3.0, F32)
        k = 0
        for dy in steps_y:
            for dz in steps_z:
                source = lax.rem(at_z + dz, 8) * 4 + lax.rem(at_y + 4 + dy, 4)
                out_ref[pl.ds(source * 2 + at_xh, 1), :] = grid[k : k + 1, :]
                k += 1


def cent_best(where, mine, other, cents, owners, cap, steps_y, steps_z):
    rows, width = mine.shape
    count = sum(c.shape[0] for c in cents)
    vmem = pl.BlockSpec(memory_space=pltpu.VMEM)
    return pl.pallas_call(
        functools.partial(cent_kernel, owners, cap, steps_y, steps_z),
        in_specs=[pl.BlockSpec(memory_space=pltpu.SMEM)] + [vmem] * (2 + len(cents)),
        out_shape=(jax.ShapeDtypeStruct((owners, cap), F32),) * 2,
        compiler_params=params(),
        cost_estimate=cost(4 * rows * count * width, (2 * rows + count) * width * 2),
    )(where, mine, other, *cents)


def block_rows(block, cap):
    blocks, deep, _ = block.shape
    pieces = (deep - NOTE) // cap
    return jnp.concatenate(
        [block[:, k * cap : (k + 1) * cap, :].reshape(blocks * cap, 128) for k in range(pieces)],
        axis=1,
    )


def block_ids(block, cap):
    blocks, deep, _ = block.shape
    notes = block[:, deep - NOTE :, :].astype(F32)[:, 0:1, :]
    sub = lax.broadcasted_iota(jnp.int32, (blocks, cap, 128), 1)
    lane = lax.broadcasted_iota(jnp.int32, (blocks, cap, 128), 2)
    spread = jnp.where(sub == lane, jnp.broadcast_to(notes, (blocks, cap, 128)), 0.0)
    return spread.reshape(blocks * cap, 128)


def dup_kernel(tiles, cap, count, with_self, first, last, own_ref, *refs):
    col_refs, refs = refs[:count], refs[count:]
    if not first:
        old_ref, refs = refs[0], refs[1:]
    out_ref, own, own_ids = refs[:3]
    acc = refs[3] if last else out_ref
    step = pl.program_id(0)
    rows = own.shape[0]

    @pl.when(step == 0)
    def _():
        acc[...] = jnp.full(acc.shape, -1.0, F32) if first else old_ref[...]
        own[...] = block_rows(own_ref[...], cap)
        own_ids[...] = jnp.sum(block_ids(own_ref[...], cap), axis=1, keepdims=True)

    for k, col_ref in enumerate(col_refs):
        block = col_ref[...]
        other = block_rows(block, cap)
        tile = other.shape[0]
        spread = block_ids(block, cap).astype(BF16)
        col_ids = dot_t(jnp.full((8, 128), 1.0, BF16), spread)[0:1, :]
        match = own_ids[...] == jnp.where(col_ids < 0, -2.0, col_ids)
        if with_self and k == 0:
            row = lax.broadcasted_iota(jnp.int32, (rows, tile), 0)
            col = lax.broadcasted_iota(jnp.int32, (rows, tile), 1) + step * tile
            match = match & (row != col)
        kept = jnp.where(match, dot_t(own[...], other), -1.0)
        best = acc[...]
        for j in range(tile // 128):
            best = jnp.maximum(best, kept[:, j * 128 : (j + 1) * 128])
        acc[...] = best

    if last:

        @pl.when(step == tiles - 1)
        def _():
            top = jnp.max(acc[...], axis=1, keepdims=True)
            out_ref[...] = column_to_grid(top, own_ref.shape[0], cap)


def dup_best(own, cols, cap, with_self=False, old=None, last=False):
    owners, deep, _ = own.shape
    rows, width = owners * cap, (deep - NOTE) // cap * 128
    each = 16
    tiles = owners // each
    whole = lambda array: pl.BlockSpec(array.shape, lambda j: (0,) * len(array.shape))
    held = jax.ShapeDtypeStruct((rows, 128), F32)
    out_shape = jax.ShapeDtypeStruct((owners, cap), F32) if last else held
    more = [] if old is None else [old]
    return pl.pallas_call(
        functools.partial(dup_kernel, tiles, cap, len(cols), with_self, old is None, last),
        grid=(tiles,),
        in_specs=[whole(own)]
        + [pl.BlockSpec((each, deep, 128), lambda j: (j, 0, 0))] * len(cols)
        + [whole(a) for a in more],
        out_specs=whole(out_shape),
        out_shape=out_shape,
        scratch_shapes=[pltpu.VMEM((rows, width), BF16), pltpu.VMEM((rows, 1), F32)]
        + ([pltpu.VMEM((rows, 128), F32)] if last else []),
        compiler_params=params(),
        cost_estimate=cost(
            2 * rows * rows * len(cols) * width, (1 + len(cols)) * rows * width * 2
        ),
    )(own, *cols, *more)


def split_kernel(cap, room, where_ref, own_ref, keep_ref, give_ref, place_ref):
    owners, deep, _ = own_ref.shape
    block = own_ref[...]
    rows = block_rows(block, cap)
    slots, width = rows.shape
    ids = block[:, deep - NOTE :, :].astype(F32)[:, 0, :]
    side = jnp.where(ids >= owners, 1.0, 0.0)
    here = where_ref[3].astype(F32)
    upper = lax.broadcasted_iota(jnp.int32, (128, 128), 0) < lax.broadcasted_iota(
        jnp.int32, (128, 128), 1
    )
    lower = lax.broadcasted_iota(jnp.int32, (owners, owners), 1) < lax.broadcasted_iota(
        jnp.int32, (owners, owners), 0
    )
    upper = jnp.where(upper, 1.0, 0.0).astype(BF16)
    lower = jnp.where(lower, 1.0, 0.0).astype(BF16)
    sub = lax.broadcasted_iota(jnp.int32, (owners, cap, 128), 1)
    lane = lax.broadcasted_iota(jnp.int32, (owners, cap, 128), 2)
    ones = jnp.full((8, 128), 1.0, BF16)
    list_row = lax.broadcasted_iota(jnp.int32, (room, slots), 0).astype(F32)

    def as_row(grid):
        wide = jnp.broadcast_to(grid.reshape(owners, 1, 128), (owners, cap, 128))
        spread = jnp.where(sub == lane, wide, 0.0).reshape(slots, 128)
        return dot_t(ones, spread.astype(BF16))[0:1, :]

    members = []
    for part, out_ref in enumerate((keep_ref, give_ref)):
        chosen = (ids >= 0) & ((side == here) if part == 0 else (side != here))
        mask = jnp.where(chosen, 1.0, 0.0)
        packed = mask.astype(BF16)
        within = jnp.dot(packed, upper, preferred_element_type=F32)
        above = jnp.sum(jnp.dot(lower, packed, preferred_element_type=F32), axis=1, keepdims=True)
        after = jnp.where(chosen, within + above + 1.0, 0.0)
        high = jnp.floor(after * (1.0 / 32.0))
        rank = 32.0 * as_row(high) + as_row(after - 32.0 * high) - 1.0
        pick = jnp.where(list_row == rank, 1.0, 0.0).astype(BF16)
        out_ref[:room, :] = jnp.dot(pick, rows, preferred_element_type=F32).astype(BF16)
        place_ref[part * owners : (part + 1) * owners, :] = after - 1.0
        members.append(jnp.sum(jnp.sum(mask, axis=1, keepdims=True), axis=0, keepdims=True))
    over = jnp.where((members[0] > room) | (members[1] > room), 1.0, 0.0)
    spot = lax.broadcasted_iota(jnp.int32, (INFO, width), 1)
    for count, out_ref in zip(members, (keep_ref, give_ref)):
        high = jnp.floor(count * (1.0 / 32.0))
        info = jnp.where(spot == 0, high, jnp.where(spot == 1, count - 32.0 * high, over))
        out_ref[room:, :] = info.astype(BF16)


def split(where, own, cap, room):
    owners, deep, _ = own.shape
    width = (deep - NOTE) // cap * 128
    rows = owners * cap
    vmem = pl.BlockSpec(memory_space=pltpu.VMEM)
    return pl.pallas_call(
        functools.partial(split_kernel, cap, room),
        in_specs=[pl.BlockSpec(memory_space=pltpu.SMEM), vmem],
        out_shape=(
            jax.ShapeDtypeStruct((room + INFO, width), BF16),
            jax.ShapeDtypeStruct((room + INFO, width), BF16),
            jax.ShapeDtypeStruct((2 * owners, 128), F32),
        ),
        compiler_params=params(),
        cost_estimate=cost(4 * rows * room * width, 3 * rows * width),
    )(where, own)


def list_kernel(room, *refs):
    list_refs, (keep_ref, came_ref) = refs[:4], refs[4:]
    over = jnp.zeros((1, 1), F32)
    counts = []
    for ref in list_refs:
        info = ref[room:, :128].astype(F32)
        counts.append(32.0 * info[0:1, 0:1] + info[0:1, 1:2])
        over = jnp.maximum(over, info[0:1, 2:3])
    other = lax.broadcasted_iota(jnp.int32, (room, room), 0)
    mine = lax.broadcasted_iota(jnp.int32, (room, room), 1)
    position = lax.broadcasted_iota(jnp.int32, (room, 1), 0).astype(F32)
    for k, out_ref in ((0, keep_ref), (1, came_ref)):
        own = list_refs[k][:room, :]
        best = jnp.full((1, room), -1.0, F32)
        for j, ref in enumerate(list_refs):
            scores = dot_t(ref[:room, :], own)
            use = position < counts[j]
            if j == k:
                use = use & (other != mine)
            best = jnp.maximum(best, jnp.max(jnp.where(use, scores, -1.0), axis=0, keepdims=True))
        out_ref[:, :room] = best
        out_ref[:, room:] = jnp.broadcast_to(over, (1, 128))


def list_best(lists, room):
    width = lists[0].shape[1]
    return pl.pallas_call(
        functools.partial(list_kernel, room),
        out_shape=(jax.ShapeDtypeStruct((1, room + 128), F32),) * 2,
        compiler_params=params(),
        cost_estimate=cost(16 * room * room * width, 8 * room * width),
    )(*lists)


def merge_kernel(owners, cap, room, kept_ref, back_ref, place_ref, mine_ref, other_ref, out_ref):
    slots = owners * cap
    sub = lax.broadcasted_iota(jnp.int32, (owners, cap, 128), 1)
    lane = lax.broadcasted_iota(jnp.int32, (owners, cap, 128), 2)
    spot = lax.broadcasted_iota(jnp.int32, (slots, room), 1).astype(F32)
    total = jnp.zeros((slots, 1), F32)
    for part, ref in enumerate((kept_ref, back_ref)):
        grid = place_ref[part * owners : (part + 1) * owners, :]
        wide = jnp.broadcast_to(grid.reshape(owners, 1, 128), (owners, cap, 128))
        spread = jnp.where(sub == lane, wide, 0.0).reshape(slots, 128)
        place = jnp.sum(spread, axis=1, keepdims=True)
        found = jnp.where(spot == place, ref[:, :room], 0.0)
        total = total + jnp.sum(found, axis=1, keepdims=True)
    out_ref[:, :cap] = column_to_grid(total, owners, cap)
    out_ref[:, cap : 2 * cap] = jnp.maximum(mine_ref[...], other_ref[...])
    out_ref[:, 2 * cap :] = jnp.broadcast_to(kept_ref[:, room : room + cap], (owners, cap))


def merge(kept, back, place, mine, other, room):
    owners, cap = mine.shape
    return pl.pallas_call(
        functools.partial(merge_kernel, owners, cap, room),
        out_shape=jax.ShapeDtypeStruct((owners, 3 * cap), F32),
        compiler_params=params(),
    )(kept, back, place, mine, other)


def unpack_kernel(owners, cap, back_ref, place_ref, dup_ref, *more_refs):
    back = back_ref[...]
    target = place_ref[0:1, :]
    rank = place_ref[1:2, :]
    rows = target.shape[1]
    found = jnp.full((owners, rows), -2.0, F32)
    for k in range(cap):
        found = jnp.where(rank == k, back[:, k : k + 1], found)
    owner_of = lax.broadcasted_iota(jnp.int32, (owners, rows), 0)
    dup_ref[...] = jnp.max(jnp.where(target == owner_of, found, -2.0), axis=0, keepdims=True)
    for k, ref in enumerate(more_refs):
        ref[...] = jnp.max(back[:, (k + 1) * cap : (k + 2) * cap], axis=0, keepdims=True)


def unpack(back, place, owners, cap):
    rows = place.shape[1]
    more = back.shape[1] // cap - 1
    return pl.pallas_call(
        functools.partial(unpack_kernel, owners, cap),
        out_shape=[jax.ShapeDtypeStruct((1, rows), F32)]
        + [jax.ShapeDtypeStruct((1, cap), F32)] * more,
        compiler_params=params(),
    )(back, place)


def join_kernel(*refs):
    out_ref, at = refs[-1], 0
    for ref in refs[:-1]:
        out_ref[at : at + ref.shape[0], :] = ref[...]
        at += ref.shape[0]


def join(*blocks):
    rows, width = sum(b.shape[0] for b in blocks), blocks[0].shape[1]
    return pl.pallas_call(
        join_kernel,
        out_shape=jax.ShapeDtypeStruct((rows, width), blocks[0].dtype),
        compiler_params=params(),
        cost_estimate=cost(0, 4 * rows * width),
    )(*blocks)


def full_scores(own, place, cap):
    owners = own.shape[0]
    own_x = lax.ppermute(own, "xl", SWAP)
    own_c = lax.ppermute(own, "c", SWAP)
    own_cx = lax.ppermute(own_x, "c", SWAP)
    held = dup_best(own, [own, own_c], cap, with_self=True)
    best = dup_best(own, [own_x, own_cx], cap, old=held, last=True)
    back = lax.all_to_all(best, OWN, split_axis=0, concat_axis=0, tiled=True)
    return unpack(back, place, owners, cap)[0]


def shards(embeddings, cluster_of, new_rows, centroids):
    owners = lax.axis_size(OWN)
    rows, width = embeddings.shape
    cap = 2 * rows // owners
    room = 3 * rows // 4
    where = jnp.stack([lax.axis_index(a) for a in (*OWN, "xl")]).astype(jnp.int32)

    cents = lax.all_gather(centroids, ("xh", "xl"), axis=0, tiled=True)
    steps_z = tuple(range(8))
    line = [new_rows] + [
        lax.ppermute(new_rows, "z", [(i, (i + 8 - k) % 8) for i in range(8)]) for k in steps_z[1:]
    ]
    send, place = pack(embeddings, cluster_of, owners, cap)
    landed = lax.all_to_all(send, OWN, split_axis=0, concat_axis=0, tiled=True)
    line = join(*line)
    own = tie(landed, cents, line)

    keep, give, spots = split(where, own, cap, room)
    came = lax.ppermute(give, "xl", SWAP)
    keep_c = lax.ppermute(keep, "c", SWAP)

    steps_y = (0, -1, 1, -2)
    line = tie(line, keep)
    left = lax.ppermute(line, "y", [(i, (i + 1) % 4) for i in range(4)])
    right = lax.ppermute(line, "y", [(i, (i + 3) % 4) for i in range(4)])
    far = lax.ppermute(left, "y", [(i, (i + 1) % 4) for i in range(4)])
    new = join(line, left, right, far)
    new_other = lax.ppermute(new, "c", SWAP)
    cent_mine, cent_theirs = cent_best(
        where, new, new_other, (cents,), owners, new_rows.shape[0], steps_y, steps_z
    )
    cent_back = lax.ppermute(cent_theirs, "c", SWAP)

    came_c = lax.ppermute(came, "c", SWAP)
    kept, guests = list_best([keep, came, keep_c, came_c], room)
    guests = lax.ppermute(guests, "xl", SWAP)
    both = merge(kept, guests, spots, cent_mine, cent_back, room)
    back = lax.all_to_all(both, OWN, split_axis=0, concat_axis=0, tiled=True)
    dup, cent_score, over = unpack(back, place, owners, cap)
    dup = lax.cond(
        over[0, 0] > 0.5,
        lambda held, spot, short: full_scores(held, spot, cap),
        lambda held, spot, short: short,
        own,
        place,
        dup,
    )
    return (dup.reshape(rows), cent_score.reshape(new_rows.shape[0]))


def solution(mesh):
    sizes = mesh.devices.shape
    owners, group = sizes
    halves = owners // 2
    inner = Mesh(mesh.devices.reshape(halves // 4, 4, 2, group // 2, 2), ALL)
    return jax.shard_map(
        shards,
        mesh=inner,
        in_specs=(P(ALL, None), P(ALL), P(ALL, None), P(ALL, None)),
        out_specs=(P(ALL), P(ALL)),
        check_vma=False,
    )
```

```python
import functools

import jax
import jax.numpy as jnp
from jax import lax
from jax.experimental import pallas as pl
from jax.experimental.pallas import tpu as pltpu
from jax.sharding import Mesh
from jax.sharding import PartitionSpec as P

EPS = 1e-06
OWN = ("z", "y", "xh")
ALL = ("z", "y", "c", "xh", "xl")
SWAP = [(0, 1), (1, 0)]
BF16 = jnp.bfloat16
F32 = jnp.float32
NOTE = 8
INFO = 16
VMEM_LIMIT = 48 * 1024 * 1024


def unit_rows(rows):
    wide = rows.astype(F32)
    total = jnp.sum(wide * wide, axis=-1, keepdims=True)
    return (wide * lax.rsqrt(total + EPS)).astype(BF16)


def dot_t(left, right):
    return lax.dot_general(left, right, (((1,), (1,)), ((), ())), preferred_element_type=F32)


def params(**kwargs):
    return pltpu.CompilerParams(vmem_limit_bytes=VMEM_LIMIT, **kwargs)


def cost(flops, moved):
    return pl.CostEstimate(flops=flops, bytes_accessed=moved, transcendentals=0)


def column_to_grid(column, owners, cap):
    wide = jnp.broadcast_to(column.reshape(owners, cap, 1), (owners, cap, 128))
    sub = lax.broadcasted_iota(jnp.int32, (owners, cap, 128), 1)
    lane = lax.broadcasted_iota(jnp.int32, (owners, cap, 128), 2)
    return jnp.sum(jnp.where(sub == lane, wide, 0.0), axis=1)[:, :cap]


def pack_kernel(cap, emb_ref, clu_ref, send_ref, place_ref):
    owners = send_ref.shape[0]
    rows, width = emb_ref.shape
    cluster = clu_ref[...]
    target = lax.rem(cluster, owners)
    owner_of = lax.broadcasted_iota(jnp.int32, (owners, rows), 0)
    hot = target == owner_of
    first = lax.broadcasted_iota(jnp.int32, (rows, rows), 0)
    second = lax.broadcasted_iota(jnp.int32, (rows, rows), 1)
    before = jnp.where(first < second, 1.0, 0.0).astype(BF16)
    ahead = jnp.dot(
        jnp.where(hot, 1.0, 0.0).astype(BF16), before, preferred_element_type=F32
    )
    rank = jnp.sum(jnp.where(hot, ahead, 0.0), axis=0, keepdims=True).astype(jnp.int32)
    place_ref[0:1, :] = target
    place_ref[1:2, :] = rank
    units = unit_rows(emb_ref[...])
    slot = target * cap + rank
    row_of = lax.broadcasted_iota(jnp.int32, (owners * cap, rows), 0)
    pick = jnp.where(row_of == slot, 1.0, 0.0).astype(BF16)
    send = jnp.dot(pick, units, preferred_element_type=F32).astype(BF16)
    for k in range(width // 128):
        piece = send[:, k * 128 : (k + 1) * 128].reshape(owners, cap, 128)
        send_ref[:, k * cap : (k + 1) * cap, :] = piece
    code = jnp.where(hot, cluster.astype(F32) + 1.0, 0.0)
    lane = lax.broadcasted_iota(jnp.int32, (owners, 128), 1)
    ids = jnp.full((owners, 128), -1.0, F32)
    for k in range(cap):
        held = jnp.sum(jnp.where(rank == k, code, 0.0), axis=1, keepdims=True)
        ids = jnp.where(lane == k, held - 1.0, ids)
    notes = jnp.broadcast_to(ids.reshape(owners, 1, 128), (owners, NOTE, 128))
    send_ref[:, width // 128 * cap :, :] = notes.astype(BF16)


def pack(emb, cluster, owners, cap):
    rows, width = emb.shape
    return pl.pallas_call(
        functools.partial(pack_kernel, cap),
        out_shape=(
            jax.ShapeDtypeStruct((owners, width // 128 * cap + NOTE, 128), BF16),
            jax.ShapeDtypeStruct((2, rows), jnp.int32),
        ),
        compiler_params=params(),
        cost_estimate=cost(2 * owners * cap * rows * width, 3 * rows * width * 2),
    )(emb, cluster.reshape(1, rows))


def tie(array, *others):
    return pl.pallas_call(
        lambda *refs: None,
        in_specs=[pl.BlockSpec(memory_space=pl.ANY)] * (1 + len(others)),
        out_specs=pl.BlockSpec(memory_space=pl.ANY),
        out_shape=jax.ShapeDtypeStruct(array.shape, array.dtype),
        input_output_aliases={0: 0},
    )(array, *others)


def unit_kernel(in_ref, out_ref):
    out_ref[...] = unit_rows(in_ref[...])


def unit(rows):
    return pl.pallas_call(
        unit_kernel,
        out_shape=jax.ShapeDtypeStruct(rows.shape, BF16),
        compiler_params=params(),
        cost_estimate=cost(4 * rows.size, 4 * rows.size),
    )(rows)


def cent_kernel(owners, cap, steps_y, steps_z, where_ref, mine_ref, other_ref, *refs):
    cent_ref, out_refs = refs[0], refs[-2:]
    at_z, at_y, at_xh = where_ref[0], where_ref[1], where_ref[2]
    for new_ref, out_ref in zip((mine_ref, other_ref), out_refs):
        new_unit = unit_rows(new_ref[...])
        best = jnp.max(dot_t(new_unit, cent_ref[...]), axis=1, keepdims=True)
        grid = column_to_grid(best, new_unit.shape[0] // cap, cap)
        out_ref[...] = jnp.full((owners, cap), -3.0, F32)
        k = 0
        for dy in steps_y:
            for dz in steps_z:
                source = lax.rem(at_z + dz, 8) * 4 + lax.rem(at_y + 4 + dy, 4)
                out_ref[pl.ds(source * 2 + at_xh, 1), :] = grid[k : k + 1, :]
                k += 1


def cent_best(where, mine, other, cents, owners, cap, steps_y, steps_z):
    rows, width = mine.shape
    count = cents.shape[0]
    vmem = pl.BlockSpec(memory_space=pltpu.VMEM)
    return pl.pallas_call(
        functools.partial(cent_kernel, owners, cap, steps_y, steps_z),
        in_specs=[pl.BlockSpec(memory_space=pltpu.SMEM)] + [vmem] * 3,
        out_shape=(jax.ShapeDtypeStruct((owners, cap), F32),) * 2,
        compiler_params=params(),
        cost_estimate=cost(4 * rows * count * width, (2 * rows + count) * width * 2),
    )(where, mine, other, cents)


def block_rows(block, cap):
    blocks, deep, _ = block.shape
    pieces = (deep - NOTE) // cap
    return jnp.concatenate(
        [block[:, k * cap : (k + 1) * cap, :].reshape(blocks * cap, 128) for k in range(pieces)],
        axis=1,
    )


def block_ids(block, cap):
    blocks, deep, _ = block.shape
    notes = block[:, deep - NOTE :, :].astype(F32)[:, 0:1, :]
    sub = lax.broadcasted_iota(jnp.int32, (blocks, cap, 128), 1)
    lane = lax.broadcasted_iota(jnp.int32, (blocks, cap, 128), 2)
    spread = jnp.where(sub == lane, jnp.broadcast_to(notes, (blocks, cap, 128)), 0.0)
    return spread.reshape(blocks * cap, 128)


def dup_kernel(tiles, cap, count, with_self, first, last, own_ref, *refs):
    col_refs, refs = refs[:count], refs[count:]
    if not first:
        old_ref, refs = refs[0], refs[1:]
    out_ref, own, own_ids = refs[:3]
    acc = refs[3] if last else out_ref
    step = pl.program_id(0)
    rows = own.shape[0]

    @pl.when(step == 0)
    def _():
        acc[...] = jnp.full(acc.shape, -1.0, F32) if first else old_ref[...]
        own[...] = block_rows(own_ref[...], cap)
        own_ids[...] = jnp.sum(block_ids(own_ref[...], cap), axis=1, keepdims=True)

    for k, col_ref in enumerate(col_refs):
        block = col_ref[...]
        other = block_rows(block, cap)
        tile = other.shape[0]
        spread = block_ids(block, cap).astype(BF16)
        col_ids = dot_t(jnp.full((8, 128), 1.0, BF16), spread)[0:1, :]
        match = own_ids[...] == jnp.where(col_ids < 0, -2.0, col_ids)
        if with_self and k == 0:
            row = lax.broadcasted_iota(jnp.int32, (rows, tile), 0)
            col = lax.broadcasted_iota(jnp.int32, (rows, tile), 1) + step * tile
            match = match & (row != col)
        kept = jnp.where(match, dot_t(own[...], other), -1.0)
        best = acc[...]
        for j in range(tile // 128):
            best = jnp.maximum(best, kept[:, j * 128 : (j + 1) * 128])
        acc[...] = best

    if last:

        @pl.when(step == tiles - 1)
        def _():
            top = jnp.max(acc[...], axis=1, keepdims=True)
            out_ref[...] = column_to_grid(top, own_ref.shape[0], cap)


def dup_best(own, cols, cap, with_self=False, old=None, last=False):
    owners, deep, _ = own.shape
    rows, width = owners * cap, (deep - NOTE) // cap * 128
    each = 16
    tiles = owners // each
    whole = lambda array: pl.BlockSpec(array.shape, lambda j: (0,) * len(array.shape))
    held = jax.ShapeDtypeStruct((rows, 128), F32)
    out_shape = jax.ShapeDtypeStruct((owners, cap), F32) if last else held
    more = [] if old is None else [old]
    return pl.pallas_call(
        functools.partial(dup_kernel, tiles, cap, len(cols), with_self, old is None, last),
        grid=(tiles,),
        in_specs=[whole(own)]
        + [pl.BlockSpec((each, deep, 128), lambda j: (j, 0, 0))] * len(cols)
        + [whole(a) for a in more],
        out_specs=whole(out_shape),
        out_shape=out_shape,
        scratch_shapes=[pltpu.VMEM((rows, width), BF16), pltpu.VMEM((rows, 1), F32)]
        + ([pltpu.VMEM((rows, 128), F32)] if last else []),
        compiler_params=params(),
        cost_estimate=cost(
            2 * rows * rows * len(cols) * width, (1 + len(cols)) * rows * width * 2
        ),
    )(own, *cols, *more)


def split_kernel(cap, room, where_ref, own_ref, keep_ref, give_ref, place_ref):
    owners, deep, _ = own_ref.shape
    block = own_ref[...]
    rows = block_rows(block, cap)
    slots, width = rows.shape
    ids = block[:, deep - NOTE :, :].astype(F32)[:, 0, :]
    side = jnp.where(ids >= owners, 1.0, 0.0)
    here = where_ref[3].astype(F32)
    upper = lax.broadcasted_iota(jnp.int32, (128, 128), 0) < lax.broadcasted_iota(
        jnp.int32, (128, 128), 1
    )
    lower = lax.broadcasted_iota(jnp.int32, (owners, owners), 1) < lax.broadcasted_iota(
        jnp.int32, (owners, owners), 0
    )
    upper = jnp.where(upper, 1.0, 0.0).astype(BF16)
    lower = jnp.where(lower, 1.0, 0.0).astype(BF16)
    sub = lax.broadcasted_iota(jnp.int32, (owners, cap, 128), 1)
    lane = lax.broadcasted_iota(jnp.int32, (owners, cap, 128), 2)
    ones = jnp.full((8, 128), 1.0, BF16)
    list_row = lax.broadcasted_iota(jnp.int32, (room, slots), 0).astype(F32)

    def as_row(grid):
        wide = jnp.broadcast_to(grid.reshape(owners, 1, 128), (owners, cap, 128))
        spread = jnp.where(sub == lane, wide, 0.0).reshape(slots, 128)
        return dot_t(ones, spread.astype(BF16))[0:1, :]

    members = []
    for part, out_ref in enumerate((keep_ref, give_ref)):
        chosen = (ids >= 0) & ((side == here) if part == 0 else (side != here))
        mask = jnp.where(chosen, 1.0, 0.0)
        packed = mask.astype(BF16)
        within = jnp.dot(packed, upper, preferred_element_type=F32)
        above = jnp.sum(jnp.dot(lower, packed, preferred_element_type=F32), axis=1, keepdims=True)
        after = jnp.where(chosen, within + above + 1.0, 0.0)
        high = jnp.floor(after * (1.0 / 32.0))
        rank = 32.0 * as_row(high) + as_row(after - 32.0 * high) - 1.0
        pick = jnp.where(list_row == rank, 1.0, 0.0).astype(BF16)
        out_ref[:room, :] = jnp.dot(pick, rows, preferred_element_type=F32).astype(BF16)
        place_ref[part * owners : (part + 1) * owners, :] = after - 1.0
        members.append(jnp.sum(jnp.sum(mask, axis=1, keepdims=True), axis=0, keepdims=True))
    over = jnp.where((members[0] > room) | (members[1] > room), 1.0, 0.0)
    spot = lax.broadcasted_iota(jnp.int32, (INFO, width), 1)
    for count, out_ref in zip(members, (keep_ref, give_ref)):
        high = jnp.floor(count * (1.0 / 32.0))
        info = jnp.where(spot == 0, high, jnp.where(spot == 1, count - 32.0 * high, over))
        out_ref[room:, :] = info.astype(BF16)


def split(where, own, cap, room):
    owners, deep, _ = own.shape
    width = (deep - NOTE) // cap * 128
    rows = owners * cap
    vmem = pl.BlockSpec(memory_space=pltpu.VMEM)
    return pl.pallas_call(
        functools.partial(split_kernel, cap, room),
        in_specs=[pl.BlockSpec(memory_space=pltpu.SMEM), vmem],
        out_shape=(
            jax.ShapeDtypeStruct((room + INFO, width), BF16),
            jax.ShapeDtypeStruct((room + INFO, width), BF16),
            jax.ShapeDtypeStruct((2 * owners, 128), F32),
        ),
        compiler_params=params(),
        cost_estimate=cost(4 * rows * room * width, 3 * rows * width),
    )(where, own)


def list_kernel(room, *refs):
    list_refs, (keep_ref, came_ref) = refs[:4], refs[4:]
    over = jnp.zeros((1, 1), F32)
    counts = []
    for ref in list_refs:
        info = ref[room:, :128].astype(F32)
        counts.append(32.0 * info[0:1, 0:1] + info[0:1, 1:2])
        over = jnp.maximum(over, info[0:1, 2:3])
    other = lax.broadcasted_iota(jnp.int32, (room, room), 0)
    mine = lax.broadcasted_iota(jnp.int32, (room, room), 1)
    position = lax.broadcasted_iota(jnp.int32, (room, 1), 0).astype(F32)
    for k, out_ref in ((0, keep_ref), (1, came_ref)):
        own = list_refs[k][:room, :]
        best = jnp.full((1, room), -1.0, F32)
        for j, ref in enumerate(list_refs):
            scores = dot_t(ref[:room, :], own)
            use = position < counts[j]
            if j == k:
                use = use & (other != mine)
            best = jnp.maximum(best, jnp.max(jnp.where(use, scores, -1.0), axis=0, keepdims=True))
        out_ref[:, :room] = best
        out_ref[:, room:] = jnp.broadcast_to(over, (1, 128))


def list_best(lists, room):
    width = lists[0].shape[1]
    return pl.pallas_call(
        functools.partial(list_kernel, room),
        out_shape=(jax.ShapeDtypeStruct((1, room + 128), F32),) * 2,
        compiler_params=params(),
        cost_estimate=cost(16 * room * room * width, 8 * room * width),
    )(*lists)


def merge_kernel(owners, cap, room, kept_ref, back_ref, place_ref, mine_ref, other_ref, out_ref):
    slots = owners * cap
    sub = lax.broadcasted_iota(jnp.int32, (owners, cap, 128), 1)
    lane = lax.broadcasted_iota(jnp.int32, (owners, cap, 128), 2)
    spot = lax.broadcasted_iota(jnp.int32, (slots, room), 1).astype(F32)
    total = jnp.zeros((slots, 1), F32)
    for part, ref in enumerate((kept_ref, back_ref)):
        grid = place_ref[part * owners : (part + 1) * owners, :]
        wide = jnp.broadcast_to(grid.reshape(owners, 1, 128), (owners, cap, 128))
        spread = jnp.where(sub == lane, wide, 0.0).reshape(slots, 128)
        place = jnp.sum(spread, axis=1, keepdims=True)
        found = jnp.where(spot == place, ref[:, :room], 0.0)
        total = total + jnp.sum(found, axis=1, keepdims=True)
    out_ref[:, :cap] = column_to_grid(total, owners, cap)
    out_ref[:, cap : 2 * cap] = jnp.maximum(mine_ref[...], other_ref[...])
    out_ref[:, 2 * cap :] = jnp.broadcast_to(kept_ref[:, room : room + cap], (owners, cap))


def merge(kept, back, place, mine, other, room):
    owners, cap = mine.shape
    return pl.pallas_call(
        functools.partial(merge_kernel, owners, cap, room),
        out_shape=jax.ShapeDtypeStruct((owners, 3 * cap), F32),
        compiler_params=params(),
    )(kept, back, place, mine, other)


def unpack_kernel(owners, cap, back_ref, place_ref, dup_ref, *more_refs):
    back = back_ref[...]
    target = place_ref[0:1, :]
    rank = place_ref[1:2, :]
    rows = target.shape[1]
    found = jnp.full((owners, rows), -2.0, F32)
    for k in range(cap):
        found = jnp.where(rank == k, back[:, k : k + 1], found)
    owner_of = lax.broadcasted_iota(jnp.int32, (owners, rows), 0)
    dup_ref[...] = jnp.max(jnp.where(target == owner_of, found, -2.0), axis=0, keepdims=True)
    for k, ref in enumerate(more_refs):
        ref[...] = jnp.max(back[:, (k + 1) * cap : (k + 2) * cap], axis=0, keepdims=True)


def unpack(back, place, owners, cap):
    rows = place.shape[1]
    more = back.shape[1] // cap - 1
    return pl.pallas_call(
        functools.partial(unpack_kernel, owners, cap),
        out_shape=[jax.ShapeDtypeStruct((1, rows), F32)]
        + [jax.ShapeDtypeStruct((1, cap), F32)] * more,
        compiler_params=params(),
    )(back, place)


def join_kernel(*refs):
    out_ref, at = refs[-1], 0
    for ref in refs[:-1]:
        out_ref[at : at + ref.shape[0], :] = ref[...]
        at += ref.shape[0]


def join(*blocks):
    rows, width = sum(b.shape[0] for b in blocks), blocks[0].shape[1]
    return pl.pallas_call(
        join_kernel,
        out_shape=jax.ShapeDtypeStruct((rows, width), blocks[0].dtype),
        compiler_params=params(),
        cost_estimate=cost(0, 4 * rows * width),
    )(*blocks)


def full_scores(own, place, cap):
    owners = own.shape[0]
    own_x = lax.ppermute(own, "xl", SWAP)
    own_c = lax.ppermute(own, "c", SWAP)
    own_cx = lax.ppermute(own_x, "c", SWAP)
    held = dup_best(own, [own, own_c], cap, with_self=True)
    best = dup_best(own, [own_x, own_cx], cap, old=held, last=True)
    back = lax.all_to_all(best, OWN, split_axis=0, concat_axis=0, tiled=True)
    return unpack(back, place, owners, cap)[0]


def shards(embeddings, cluster_of, new_rows, centroids):
    owners = lax.axis_size(OWN)
    rows, width = embeddings.shape
    cap = 2 * rows // owners
    room = 3 * rows // 4
    where = jnp.stack([lax.axis_index(a) for a in (*OWN, "xl")]).astype(jnp.int32)

    cents = lax.all_gather(unit(centroids), ("xh", "xl"), axis=0, tiled=True)
    steps_z = tuple(range(8))
    line = [new_rows] + [
        lax.ppermute(new_rows, "z", [(i, (i + 8 - k) % 8) for i in range(8)]) for k in steps_z[1:]
    ]
    send, place = pack(embeddings, cluster_of, owners, cap)
    landed = lax.all_to_all(send, OWN, split_axis=0, concat_axis=0, tiled=True)
    line = join(*line)
    own = tie(landed, cents, line)

    keep, give, spots = split(where, own, cap, room)
    came = lax.ppermute(give, "xl", SWAP)
    keep_c = lax.ppermute(keep, "c", SWAP)

    steps_y = (0, -1, 1, -2)
    line = tie(line, keep)
    left = lax.ppermute(line, "y", [(i, (i + 1) % 4) for i in range(4)])
    right = lax.ppermute(line, "y", [(i, (i + 3) % 4) for i in range(4)])
    far = lax.ppermute(line, "y", [(i, (i + 2) % 4) for i in range(4)])
    new = join(line, left, right, far)
    new_other = lax.ppermute(new, "c", SWAP)
    cent_mine, cent_theirs = cent_best(
        where, new, new_other, cents, owners, new_rows.shape[0], steps_y, steps_z
    )
    cent_back = lax.ppermute(cent_theirs, "c", SWAP)

    came_c = lax.ppermute(came, "c", SWAP)
    kept, guests = list_best([keep, came, keep_c, came_c], room)
    guests = lax.ppermute(guests, "xl", SWAP)
    both = merge(kept, guests, spots, cent_mine, cent_back, room)
    back = lax.all_to_all(both, OWN, split_axis=0, concat_axis=0, tiled=True)
    dup, cent_score, over = unpack(back, place, owners, cap)
    dup = lax.cond(
        over[0, 0] > 0.5,
        lambda held, spot, short: full_scores(held, spot, cap),
        lambda held, spot, short: short,
        own,
        place,
        dup,
    )
    return (dup.reshape(rows), cent_score.reshape(new_rows.shape[0]))


def solution(mesh):
    sizes = mesh.devices.shape
    owners, group = sizes
    halves = owners // 2
    inner = Mesh(mesh.devices.reshape(halves // 4, 4, 2, group // 2, 2), ALL)
    return jax.shard_map(
        shards,
        mesh=inner,
        in_specs=(P(ALL, None), P(ALL), P(ALL, None), P(ALL, None)),
        out_specs=(P(ALL), P(ALL)),
        check_vma=False,
    )
```

```python
import functools

import jax
import jax.numpy as jnp
from jax import lax
from jax.experimental import pallas as pl
from jax.experimental.pallas import tpu as pltpu
from jax.sharding import Mesh
from jax.sharding import PartitionSpec as P

EPS = 1e-06
OWN = ("z", "y", "xh")
ALL = ("z", "y", "c", "xh", "xl")
SWAP = [(0, 1), (1, 0)]
BF16 = jnp.bfloat16
F32 = jnp.float32
NOTE = 8
INFO = 16
VMEM_LIMIT = 48 * 1024 * 1024


def unit_rows(rows):
    wide = rows.astype(F32)
    total = jnp.sum(wide * wide, axis=-1, keepdims=True)
    return (wide * lax.rsqrt(total + EPS)).astype(BF16)


def dot_t(left, right):
    return lax.dot_general(left, right, (((1,), (1,)), ((), ())), preferred_element_type=F32)


def params(**kwargs):
    return pltpu.CompilerParams(vmem_limit_bytes=VMEM_LIMIT, **kwargs)


def cost(flops, moved):
    return pl.CostEstimate(flops=flops, bytes_accessed=moved, transcendentals=0)


def column_to_grid(column, owners, cap):
    wide = jnp.broadcast_to(column.reshape(owners, cap, 1), (owners, cap, 128))
    sub = lax.broadcasted_iota(jnp.int32, (owners, cap, 128), 1)
    lane = lax.broadcasted_iota(jnp.int32, (owners, cap, 128), 2)
    return jnp.sum(jnp.where(sub == lane, wide, 0.0), axis=1)[:, :cap]


def pack_kernel(cap, emb_ref, clu_ref, send_ref, place_ref):
    owners = send_ref.shape[0]
    rows, width = emb_ref.shape
    cluster = clu_ref[...]
    target = lax.rem(cluster, owners)
    owner_of = lax.broadcasted_iota(jnp.int32, (owners, rows), 0)
    hot = target == owner_of
    first = lax.broadcasted_iota(jnp.int32, (rows, rows), 0)
    second = lax.broadcasted_iota(jnp.int32, (rows, rows), 1)
    before = jnp.where(first < second, 1.0, 0.0).astype(BF16)
    ahead = jnp.dot(
        jnp.where(hot, 1.0, 0.0).astype(BF16), before, preferred_element_type=F32
    )
    rank = jnp.sum(jnp.where(hot, ahead, 0.0), axis=0, keepdims=True).astype(jnp.int32)
    place_ref[0:1, :] = target
    place_ref[1:2, :] = rank
    units = unit_rows(emb_ref[...])
    slot = target * cap + rank
    row_of = lax.broadcasted_iota(jnp.int32, (owners * cap, rows), 0)
    pick = jnp.where(row_of == slot, 1.0, 0.0).astype(BF16)
    send = jnp.dot(pick, units, preferred_element_type=F32).astype(BF16)
    for k in range(width // 128):
        piece = send[:, k * 128 : (k + 1) * 128].reshape(owners, cap, 128)
        send_ref[:, k * cap : (k + 1) * cap, :] = piece
    code = jnp.where(hot, cluster.astype(F32) + 1.0, 0.0)
    lane = lax.broadcasted_iota(jnp.int32, (owners, 128), 1)
    ids = jnp.full((owners, 128), -1.0, F32)
    for k in range(cap):
        held = jnp.sum(jnp.where(rank == k, code, 0.0), axis=1, keepdims=True)
        ids = jnp.where(lane == k, held - 1.0, ids)
    notes = jnp.broadcast_to(ids.reshape(owners, 1, 128), (owners, NOTE, 128))
    send_ref[:, width // 128 * cap :, :] = notes.astype(BF16)


def pack(emb, cluster, owners, cap):
    rows, width = emb.shape
    return pl.pallas_call(
        functools.partial(pack_kernel, cap),
        out_shape=(
            jax.ShapeDtypeStruct((owners, width // 128 * cap + NOTE, 128), BF16),
            jax.ShapeDtypeStruct((2, rows), jnp.int32),
        ),
        compiler_params=params(),
        cost_estimate=cost(2 * owners * cap * rows * width, 3 * rows * width * 2),
    )(emb, cluster.reshape(1, rows))


def tie(array, *others):
    return pl.pallas_call(
        lambda *refs: None,
        in_specs=[pl.BlockSpec(memory_space=pl.ANY)] * (1 + len(others)),
        out_specs=pl.BlockSpec(memory_space=pl.ANY),
        out_shape=jax.ShapeDtypeStruct(array.shape, array.dtype),
        input_output_aliases={0: 0},
    )(array, *others)


def unit_kernel(in_ref, out_ref):
    out_ref[...] = unit_rows(in_ref[...])


def unit(rows):
    return pl.pallas_call(
        unit_kernel,
        out_shape=jax.ShapeDtypeStruct(rows.shape, BF16),
        compiler_params=params(),
        cost_estimate=cost(4 * rows.size, 4 * rows.size),
    )(rows)


def cent_kernel(owners, cap, steps_y, steps_z, where_ref, mine_ref, other_ref, *refs):
    cent_ref, out_refs = refs[0], refs[-2:]
    at_z, at_y, at_xh = where_ref[0], where_ref[1], where_ref[2]
    for new_ref, out_ref in zip((mine_ref, other_ref), out_refs):
        new_unit = unit_rows(new_ref[...])
        best = jnp.max(dot_t(new_unit, cent_ref[...]), axis=1, keepdims=True)
        grid = column_to_grid(best, new_unit.shape[0] // cap, cap)
        out_ref[...] = jnp.full((owners, cap), -3.0, F32)
        k = 0
        for dy in steps_y:
            for dz in steps_z:
                source = lax.rem(at_z + dz, 8) * 4 + lax.rem(at_y + 4 + dy, 4)
                out_ref[pl.ds(source * 2 + at_xh, 1), :] = grid[k : k + 1, :]
                k += 1


def cent_best(where, mine, other, cents, owners, cap, steps_y, steps_z):
    rows, width = mine.shape
    count = cents.shape[0]
    vmem = pl.BlockSpec(memory_space=pltpu.VMEM)
    return pl.pallas_call(
        functools.partial(cent_kernel, owners, cap, steps_y, steps_z),
        in_specs=[pl.BlockSpec(memory_space=pltpu.SMEM)] + [vmem] * 3,
        out_shape=(jax.ShapeDtypeStruct((owners, cap), F32),) * 2,
        compiler_params=params(),
        cost_estimate=cost(4 * rows * count * width, (2 * rows + count) * width * 2),
    )(where, mine, other, cents)


def block_rows(block, cap):
    blocks, deep, _ = block.shape
    pieces = (deep - NOTE) // cap
    return jnp.concatenate(
        [block[:, k * cap : (k + 1) * cap, :].reshape(blocks * cap, 128) for k in range(pieces)],
        axis=1,
    )


def block_ids(block, cap):
    blocks, deep, _ = block.shape
    notes = block[:, deep - NOTE :, :].astype(F32)[:, 0:1, :]
    sub = lax.broadcasted_iota(jnp.int32, (blocks, cap, 128), 1)
    lane = lax.broadcasted_iota(jnp.int32, (blocks, cap, 128), 2)
    spread = jnp.where(sub == lane, jnp.broadcast_to(notes, (blocks, cap, 128)), 0.0)
    return spread.reshape(blocks * cap, 128)


def dup_kernel(tiles, cap, count, with_self, first, last, own_ref, *refs):
    col_refs, refs = refs[:count], refs[count:]
    if not first:
        old_ref, refs = refs[0], refs[1:]
    out_ref, own, own_ids = refs[:3]
    acc = refs[3] if last else out_ref
    step = pl.program_id(0)
    rows = own.shape[0]

    @pl.when(step == 0)
    def _():
        acc[...] = jnp.full(acc.shape, -1.0, F32) if first else old_ref[...]
        own[...] = block_rows(own_ref[...], cap)
        own_ids[...] = jnp.sum(block_ids(own_ref[...], cap), axis=1, keepdims=True)

    for k, col_ref in enumerate(col_refs):
        block = col_ref[...]
        other = block_rows(block, cap)
        tile = other.shape[0]
        spread = block_ids(block, cap).astype(BF16)
        col_ids = dot_t(jnp.full((8, 128), 1.0, BF16), spread)[0:1, :]
        match = own_ids[...] == jnp.where(col_ids < 0, -2.0, col_ids)
        if with_self and k == 0:
            row = lax.broadcasted_iota(jnp.int32, (rows, tile), 0)
            col = lax.broadcasted_iota(jnp.int32, (rows, tile), 1) + step * tile
            match = match & (row != col)
        kept = jnp.where(match, dot_t(own[...], other), -1.0)
        best = acc[...]
        for j in range(tile // 128):
            best = jnp.maximum(best, kept[:, j * 128 : (j + 1) * 128])
        acc[...] = best

    if last:

        @pl.when(step == tiles - 1)
        def _():
            top = jnp.max(acc[...], axis=1, keepdims=True)
            out_ref[...] = column_to_grid(top, own_ref.shape[0], cap)


def dup_best(own, cols, cap, with_self=False, old=None, last=False):
    owners, deep, _ = own.shape
    rows, width = owners * cap, (deep - NOTE) // cap * 128
    each = 16
    tiles = owners // each
    whole = lambda array: pl.BlockSpec(array.shape, lambda j: (0,) * len(array.shape))
    held = jax.ShapeDtypeStruct((rows, 128), F32)
    out_shape = jax.ShapeDtypeStruct((owners, cap), F32) if last else held
    more = [] if old is None else [old]
    return pl.pallas_call(
        functools.partial(dup_kernel, tiles, cap, len(cols), with_self, old is None, last),
        grid=(tiles,),
        in_specs=[whole(own)]
        + [pl.BlockSpec((each, deep, 128), lambda j: (j, 0, 0))] * len(cols)
        + [whole(a) for a in more],
        out_specs=whole(out_shape),
        out_shape=out_shape,
        scratch_shapes=[pltpu.VMEM((rows, width), BF16), pltpu.VMEM((rows, 1), F32)]
        + ([pltpu.VMEM((rows, 128), F32)] if last else []),
        compiler_params=params(),
        cost_estimate=cost(
            2 * rows * rows * len(cols) * width, (1 + len(cols)) * rows * width * 2
        ),
    )(own, *cols, *more)


def split_kernel(cap, room, where_ref, own_ref, keep_ref, give_ref, place_ref):
    owners, deep, _ = own_ref.shape
    block = own_ref[...]
    rows = block_rows(block, cap)
    slots, width = rows.shape
    ids = block[:, deep - NOTE :, :].astype(F32)[:, 0, :]
    side = jnp.where(ids >= owners, 1.0, 0.0)
    here = where_ref[3].astype(F32)
    upper = lax.broadcasted_iota(jnp.int32, (128, 128), 0) < lax.broadcasted_iota(
        jnp.int32, (128, 128), 1
    )
    lower = lax.broadcasted_iota(jnp.int32, (owners, owners), 1) < lax.broadcasted_iota(
        jnp.int32, (owners, owners), 0
    )
    upper = jnp.where(upper, 1.0, 0.0).astype(BF16)
    lower = jnp.where(lower, 1.0, 0.0).astype(BF16)
    sub = lax.broadcasted_iota(jnp.int32, (owners, cap, 128), 1)
    lane = lax.broadcasted_iota(jnp.int32, (owners, cap, 128), 2)
    ones = jnp.full((8, 128), 1.0, BF16)
    list_row = lax.broadcasted_iota(jnp.int32, (room, slots), 0).astype(F32)

    def as_row(grid):
        wide = jnp.broadcast_to(grid.reshape(owners, 1, 128), (owners, cap, 128))
        spread = jnp.where(sub == lane, wide, 0.0).reshape(slots, 128)
        return dot_t(ones, spread.astype(BF16))[0:1, :]

    members = []
    for part, out_ref in enumerate((keep_ref, give_ref)):
        chosen = (ids >= 0) & ((side == here) if part == 0 else (side != here))
        mask = jnp.where(chosen, 1.0, 0.0)
        packed = mask.astype(BF16)
        within = jnp.dot(packed, upper, preferred_element_type=F32)
        above = jnp.sum(jnp.dot(lower, packed, preferred_element_type=F32), axis=1, keepdims=True)
        after = jnp.where(chosen, within + above + 1.0, 0.0)
        high = jnp.floor(after * (1.0 / 32.0))
        rank = 32.0 * as_row(high) + as_row(after - 32.0 * high) - 1.0
        pick = jnp.where(list_row == rank, 1.0, 0.0).astype(BF16)
        out_ref[:room, :] = jnp.dot(pick, rows, preferred_element_type=F32).astype(BF16)
        place_ref[part * owners : (part + 1) * owners, :] = after - 1.0
        members.append(jnp.sum(jnp.sum(mask, axis=1, keepdims=True), axis=0, keepdims=True))
    over = jnp.where((members[0] > room) | (members[1] > room), 1.0, 0.0)
    spot = lax.broadcasted_iota(jnp.int32, (INFO, width), 1)
    for count, out_ref in zip(members, (keep_ref, give_ref)):
        high = jnp.floor(count * (1.0 / 32.0))
        info = jnp.where(spot == 0, high, jnp.where(spot == 1, count - 32.0 * high, over))
        out_ref[room:, :] = info.astype(BF16)


def split(where, own, cap, room):
    owners, deep, _ = own.shape
    width = (deep - NOTE) // cap * 128
    rows = owners * cap
    vmem = pl.BlockSpec(memory_space=pltpu.VMEM)
    return pl.pallas_call(
        functools.partial(split_kernel, cap, room),
        in_specs=[pl.BlockSpec(memory_space=pltpu.SMEM), vmem],
        out_shape=(
            jax.ShapeDtypeStruct((room + INFO, width), BF16),
            jax.ShapeDtypeStruct((room + INFO, width), BF16),
            jax.ShapeDtypeStruct((2 * owners, 128), F32),
        ),
        compiler_params=params(),
        cost_estimate=cost(4 * rows * room * width, 3 * rows * width),
    )(where, own)


def list_kernel(room, *refs):
    list_refs, (keep_ref, came_ref) = refs[:4], refs[4:]
    over = jnp.zeros((1, 1), F32)
    counts = []
    for ref in list_refs:
        info = ref[room:, :128].astype(F32)
        counts.append(32.0 * info[0:1, 0:1] + info[0:1, 1:2])
        over = jnp.maximum(over, info[0:1, 2:3])
    other = lax.broadcasted_iota(jnp.int32, (room, room), 0)
    mine = lax.broadcasted_iota(jnp.int32, (room, room), 1)
    position = lax.broadcasted_iota(jnp.int32, (room, 1), 0).astype(F32)
    for k, out_ref in ((0, keep_ref), (1, came_ref)):
        own = list_refs[k][:room, :]
        best = jnp.full((1, room), -1.0, F32)
        for j, ref in enumerate(list_refs):
            scores = dot_t(ref[:room, :], own)
            use = position < counts[j]
            if j == k:
                use = use & (other != mine)
            best = jnp.maximum(best, jnp.max(jnp.where(use, scores, -1.0), axis=0, keepdims=True))
        out_ref[:, :room] = best
        out_ref[:, room:] = jnp.broadcast_to(over, (1, 128))


def list_best(lists, room):
    width = lists[0].shape[1]
    return pl.pallas_call(
        functools.partial(list_kernel, room),
        out_shape=(jax.ShapeDtypeStruct((1, room + 128), F32),) * 2,
        compiler_params=params(),
        cost_estimate=cost(16 * room * room * width, 8 * room * width),
    )(*lists)


def merge_kernel(owners, cap, room, kept_ref, back_ref, place_ref, mine_ref, other_ref, out_ref):
    slots = owners * cap
    sub = lax.broadcasted_iota(jnp.int32, (owners, cap, 128), 1)
    lane = lax.broadcasted_iota(jnp.int32, (owners, cap, 128), 2)
    spot = lax.broadcasted_iota(jnp.int32, (slots, room), 1).astype(F32)
    total = jnp.zeros((slots, 1), F32)
    for part, ref in enumerate((kept_ref, back_ref)):
        grid = place_ref[part * owners : (part + 1) * owners, :]
        wide = jnp.broadcast_to(grid.reshape(owners, 1, 128), (owners, cap, 128))
        spread = jnp.where(sub == lane, wide, 0.0).reshape(slots, 128)
        place = jnp.sum(spread, axis=1, keepdims=True)
        found = jnp.where(spot == place, ref[:, :room], 0.0)
        total = total + jnp.sum(found, axis=1, keepdims=True)
    out_ref[:, :cap] = column_to_grid(total, owners, cap)
    out_ref[:, cap : 2 * cap] = jnp.maximum(mine_ref[...], other_ref[...])
    out_ref[:, 2 * cap :] = jnp.broadcast_to(kept_ref[:, room : room + cap], (owners, cap))


def merge(kept, back, place, mine, other, room):
    owners, cap = mine.shape
    return pl.pallas_call(
        functools.partial(merge_kernel, owners, cap, room),
        out_shape=jax.ShapeDtypeStruct((owners, 3 * cap), F32),
        compiler_params=params(),
    )(kept, back, place, mine, other)


def unpack_kernel(owners, cap, back_ref, place_ref, dup_ref, *more_refs):
    back = back_ref[...]
    target = place_ref[0:1, :]
    rank = place_ref[1:2, :]
    rows = target.shape[1]
    found = jnp.full((owners, rows), -2.0, F32)
    for k in range(cap):
        found = jnp.where(rank == k, back[:, k : k + 1], found)
    owner_of = lax.broadcasted_iota(jnp.int32, (owners, rows), 0)
    dup_ref[...] = jnp.max(jnp.where(target == owner_of, found, -2.0), axis=0, keepdims=True)
    for k, ref in enumerate(more_refs):
        ref[...] = jnp.max(back[:, (k + 1) * cap : (k + 2) * cap], axis=0, keepdims=True)


def unpack(back, place, owners, cap):
    rows = place.shape[1]
    more = back.shape[1] // cap - 1
    return pl.pallas_call(
        functools.partial(unpack_kernel, owners, cap),
        out_shape=[jax.ShapeDtypeStruct((1, rows), F32)]
        + [jax.ShapeDtypeStruct((1, cap), F32)] * more,
        compiler_params=params(),
    )(back, place)


def join_kernel(*refs):
    out_ref, at = refs[-1], 0
    for ref in refs[:-1]:
        out_ref[at : at + ref.shape[0], :] = ref[...]
        at += ref.shape[0]


def join(*blocks):
    rows, width = sum(b.shape[0] for b in blocks), blocks[0].shape[1]
    return pl.pallas_call(
        join_kernel,
        out_shape=jax.ShapeDtypeStruct((rows, width), blocks[0].dtype),
        compiler_params=params(),
        cost_estimate=cost(0, 4 * rows * width),
    )(*blocks)


def full_scores(own, place, cap):
    owners = own.shape[0]
    own_x = lax.ppermute(own, "xl", SWAP)
    own_c = lax.ppermute(own, "c", SWAP)
    own_cx = lax.ppermute(own_x, "c", SWAP)
    held = dup_best(own, [own, own_c], cap, with_self=True)
    best = dup_best(own, [own_x, own_cx], cap, old=held, last=True)
    back = lax.all_to_all(best, OWN, split_axis=0, concat_axis=0, tiled=True)
    return unpack(back, place, owners, cap)[0]


def moved(block, axis, size, by):
    return lax.ppermute(block, axis, [(i, (i - by) % size) for i in range(size)])


def shards(embeddings, cluster_of, new_rows, centroids):
    owners = lax.axis_size(OWN)
    rows, width = embeddings.shape
    cap = 2 * rows // owners
    room = 3 * rows // 4
    where = jnp.stack([lax.axis_index(a) for a in (*OWN, "xl")]).astype(jnp.int32)

    cents = lax.all_gather(unit(centroids), ("xh", "xl"), axis=0, tiled=True)
    line = join(new_rows, *(moved(new_rows, "z", 8, k) for k in (2, 4, 6)))
    steps_z = (0, 2, 4, 6, 1, 3, 5, 7)
    send, place = pack(embeddings, cluster_of, owners, cap)
    landed = lax.all_to_all(send, OWN, split_axis=0, concat_axis=0, tiled=True)
    own = tie(landed, cents, line)

    keep, give, spots = split(where, own, cap, room)
    came = lax.ppermute(give, "xl", SWAP)
    keep_c = lax.ppermute(keep, "c", SWAP)

    steps_y = (0, -1, 1, -2)
    line = join(line, moved(line, "z", 8, 1))
    left = lax.ppermute(line, "y", [(i, (i + 1) % 4) for i in range(4)])
    right = lax.ppermute(line, "y", [(i, (i + 3) % 4) for i in range(4)])
    far = lax.ppermute(line, "y", [(i, (i + 2) % 4) for i in range(4)])
    new = join(line, left, right, far)
    new_other = lax.ppermute(new, "c", SWAP)
    cent_mine, cent_theirs = cent_best(
        where, new, new_other, cents, owners, new_rows.shape[0], steps_y, steps_z
    )
    cent_back = lax.ppermute(cent_theirs, "c", SWAP)

    came_c = lax.ppermute(came, "c", SWAP)
    kept, guests = list_best([keep, came, keep_c, came_c], room)
    guests = lax.ppermute(guests, "xl", SWAP)
    both = merge(kept, guests, spots, cent_mine, cent_back, room)
    back = lax.all_to_all(both, OWN, split_axis=0, concat_axis=0, tiled=True)
    dup, cent_score, over = unpack(back, place, owners, cap)
    dup = lax.cond(
        over[0, 0] > 0.5,
        lambda held, spot, short: full_scores(held, spot, cap),
        lambda held, spot, short: short,
        own,
        place,
        dup,
    )
    return (dup.reshape(rows), cent_score.reshape(new_rows.shape[0]))


def solution(mesh):
    sizes = mesh.devices.shape
    owners, group = sizes
    halves = owners // 2
    inner = Mesh(mesh.devices.reshape(halves // 4, 4, 2, group // 2, 2), ALL)
    return jax.shard_map(
        shards,
        mesh=inner,
        in_specs=(P(ALL, None), P(ALL), P(ALL, None), P(ALL, None)),
        out_specs=(P(ALL), P(ALL)),
        check_vma=False,
    )
```

```python
import functools

import jax
import jax.numpy as jnp
from jax import lax
from jax.experimental import pallas as pl
from jax.experimental.pallas import tpu as pltpu
from jax.sharding import Mesh
from jax.sharding import PartitionSpec as P

EPS = 1e-06
OWN = ("z", "y", "xh")
ALL = ("z", "y", "c", "xh", "xl")
SWAP = [(0, 1), (1, 0)]
BF16 = jnp.bfloat16
F32 = jnp.float32
NOTE = 8
INFO = 16
VMEM_LIMIT = 48 * 1024 * 1024


def unit_rows(rows):
    wide = rows.astype(F32)
    total = jnp.sum(wide * wide, axis=-1, keepdims=True)
    return (wide * lax.rsqrt(total + EPS)).astype(BF16)


def dot_t(left, right):
    return lax.dot_general(left, right, (((1,), (1,)), ((), ())), preferred_element_type=F32)


def params(**kwargs):
    return pltpu.CompilerParams(vmem_limit_bytes=VMEM_LIMIT, **kwargs)


def cost(flops, moved):
    return pl.CostEstimate(flops=flops, bytes_accessed=moved, transcendentals=0)


def column_to_grid(column, owners, cap):
    wide = jnp.broadcast_to(column.reshape(owners, cap, 1), (owners, cap, 128))
    sub = lax.broadcasted_iota(jnp.int32, (owners, cap, 128), 1)
    lane = lax.broadcasted_iota(jnp.int32, (owners, cap, 128), 2)
    return jnp.sum(jnp.where(sub == lane, wide, 0.0), axis=1)[:, :cap]


def pack_kernel(cap, emb_ref, clu_ref, send_ref, place_ref):
    owners = send_ref.shape[0]
    rows, width = emb_ref.shape
    cluster = clu_ref[...]
    target = lax.rem(cluster, owners)
    owner_of = lax.broadcasted_iota(jnp.int32, (owners, rows), 0)
    hot = target == owner_of
    first = lax.broadcasted_iota(jnp.int32, (rows, rows), 0)
    second = lax.broadcasted_iota(jnp.int32, (rows, rows), 1)
    before = jnp.where(first < second, 1.0, 0.0).astype(BF16)
    ahead = jnp.dot(
        jnp.where(hot, 1.0, 0.0).astype(BF16), before, preferred_element_type=F32
    )
    rank = jnp.sum(jnp.where(hot, ahead, 0.0), axis=0, keepdims=True).astype(jnp.int32)
    place_ref[0:1, :] = target
    place_ref[1:2, :] = rank
    units = unit_rows(emb_ref[...])
    slot = target * cap + rank
    row_of = lax.broadcasted_iota(jnp.int32, (owners * cap, rows), 0)
    pick = jnp.where(row_of == slot, 1.0, 0.0).astype(BF16)
    send = jnp.dot(pick, units, preferred_element_type=F32).astype(BF16)
    for k in range(width // 128):
        piece = send[:, k * 128 : (k + 1) * 128].reshape(owners, cap, 128)
        send_ref[:, k * cap : (k + 1) * cap, :] = piece
    code = jnp.where(hot, cluster.astype(F32) + 1.0, 0.0)
    lane = lax.broadcasted_iota(jnp.int32, (owners, 128), 1)
    ids = jnp.full((owners, 128), -1.0, F32)
    for k in range(cap):
        held = jnp.sum(jnp.where(rank == k, code, 0.0), axis=1, keepdims=True)
        ids = jnp.where(lane == k, held - 1.0, ids)
    notes = jnp.broadcast_to(ids.reshape(owners, 1, 128), (owners, NOTE, 128))
    send_ref[:, width // 128 * cap :, :] = notes.astype(BF16)


def pack(emb, cluster, owners, cap):
    rows, width = emb.shape
    return pl.pallas_call(
        functools.partial(pack_kernel, cap),
        out_shape=(
            jax.ShapeDtypeStruct((owners, width // 128 * cap + NOTE, 128), BF16),
            jax.ShapeDtypeStruct((2, rows), jnp.int32),
        ),
        compiler_params=params(),
        cost_estimate=cost(2 * owners * cap * rows * width, 3 * rows * width * 2),
    )(emb, cluster.reshape(1, rows))


def tie(array, *others):
    return pl.pallas_call(
        lambda *refs: None,
        in_specs=[pl.BlockSpec(memory_space=pl.ANY)] * (1 + len(others)),
        out_specs=pl.BlockSpec(memory_space=pl.ANY),
        out_shape=jax.ShapeDtypeStruct(array.shape, array.dtype),
        input_output_aliases={0: 0},
    )(array, *others)


def unit_kernel(in_ref, out_ref):
    out_ref[...] = unit_rows(in_ref[...])


def unit(rows):
    return pl.pallas_call(
        unit_kernel,
        out_shape=jax.ShapeDtypeStruct(rows.shape, BF16),
        compiler_params=params(),
        cost_estimate=cost(4 * rows.size, 4 * rows.size),
    )(rows)


def cent_kernel(owners, cap, steps_y, steps_z, where_ref, mine_ref, other_ref, *refs):
    cent_ref, out_refs = refs[0], refs[-2:]
    at_z, at_y, at_xh = where_ref[0], where_ref[1], where_ref[2]
    for new_ref, out_ref in zip((mine_ref, other_ref), out_refs):
        new_unit = unit_rows(new_ref[...])
        best = jnp.max(dot_t(new_unit, cent_ref[...]), axis=1, keepdims=True)
        grid = column_to_grid(best, new_unit.shape[0] // cap, cap)
        out_ref[...] = jnp.full((owners, cap), -3.0, F32)
        k = 0
        for dy in steps_y:
            for dz in steps_z:
                source = lax.rem(at_z + dz, 8) * 4 + lax.rem(at_y + 4 + dy, 4)
                out_ref[pl.ds(source * 2 + at_xh, 1), :] = grid[k : k + 1, :]
                k += 1


def cent_best(where, mine, other, cents, owners, cap, steps_y, steps_z):
    rows, width = mine.shape
    count = cents.shape[0]
    vmem = pl.BlockSpec(memory_space=pltpu.VMEM)
    return pl.pallas_call(
        functools.partial(cent_kernel, owners, cap, steps_y, steps_z),
        in_specs=[pl.BlockSpec(memory_space=pltpu.SMEM)] + [vmem] * 3,
        out_shape=(jax.ShapeDtypeStruct((owners, cap), F32),) * 2,
        compiler_params=params(),
        cost_estimate=cost(4 * rows * count * width, (2 * rows + count) * width * 2),
    )(where, mine, other, cents)


def block_rows(block, cap):
    blocks, deep, _ = block.shape
    pieces = (deep - NOTE) // cap
    return jnp.concatenate(
        [block[:, k * cap : (k + 1) * cap, :].reshape(blocks * cap, 128) for k in range(pieces)],
        axis=1,
    )


def block_ids(block, cap):
    blocks, deep, _ = block.shape
    notes = block[:, deep - NOTE :, :].astype(F32)[:, 0:1, :]
    sub = lax.broadcasted_iota(jnp.int32, (blocks, cap, 128), 1)
    lane = lax.broadcasted_iota(jnp.int32, (blocks, cap, 128), 2)
    spread = jnp.where(sub == lane, jnp.broadcast_to(notes, (blocks, cap, 128)), 0.0)
    return spread.reshape(blocks * cap, 128)


def dup_kernel(tiles, cap, count, with_self, first, last, own_ref, *refs):
    col_refs, refs = refs[:count], refs[count:]
    if not first:
        old_ref, refs = refs[0], refs[1:]
    out_ref, own, own_ids = refs[:3]
    acc = refs[3] if last else out_ref
    step = pl.program_id(0)
    rows = own.shape[0]

    @pl.when(step == 0)
    def _():
        acc[...] = jnp.full(acc.shape, -1.0, F32) if first else old_ref[...]
        own[...] = block_rows(own_ref[...], cap)
        own_ids[...] = jnp.sum(block_ids(own_ref[...], cap), axis=1, keepdims=True)

    for k, col_ref in enumerate(col_refs):
        block = col_ref[...]
        other = block_rows(block, cap)
        tile = other.shape[0]
        spread = block_ids(block, cap).astype(BF16)
        col_ids = dot_t(jnp.full((8, 128), 1.0, BF16), spread)[0:1, :]
        match = own_ids[...] == jnp.where(col_ids < 0, -2.0, col_ids)
        if with_self and k == 0:
            row = lax.broadcasted_iota(jnp.int32, (rows, tile), 0)
            col = lax.broadcasted_iota(jnp.int32, (rows, tile), 1) + step * tile
            match = match & (row != col)
        kept = jnp.where(match, dot_t(own[...], other), -1.0)
        best = acc[...]
        for j in range(tile // 128):
            best = jnp.maximum(best, kept[:, j * 128 : (j + 1) * 128])
        acc[...] = best

    if last:

        @pl.when(step == tiles - 1)
        def _():
            top = jnp.max(acc[...], axis=1, keepdims=True)
            out_ref[...] = column_to_grid(top, own_ref.shape[0], cap)


def dup_best(own, cols, cap, with_self=False, old=None, last=False):
    owners, deep, _ = own.shape
    rows, width = owners * cap, (deep - NOTE) // cap * 128
    each = 16
    tiles = owners // each
    whole = lambda array: pl.BlockSpec(array.shape, lambda j: (0,) * len(array.shape))
    held = jax.ShapeDtypeStruct((rows, 128), F32)
    out_shape = jax.ShapeDtypeStruct((owners, cap), F32) if last else held
    more = [] if old is None else [old]
    return pl.pallas_call(
        functools.partial(dup_kernel, tiles, cap, len(cols), with_self, old is None, last),
        grid=(tiles,),
        in_specs=[whole(own)]
        + [pl.BlockSpec((each, deep, 128), lambda j: (j, 0, 0))] * len(cols)
        + [whole(a) for a in more],
        out_specs=whole(out_shape),
        out_shape=out_shape,
        scratch_shapes=[pltpu.VMEM((rows, width), BF16), pltpu.VMEM((rows, 1), F32)]
        + ([pltpu.VMEM((rows, 128), F32)] if last else []),
        compiler_params=params(),
        cost_estimate=cost(
            2 * rows * rows * len(cols) * width, (1 + len(cols)) * rows * width * 2
        ),
    )(own, *cols, *more)


def split_kernel(cap, room, where_ref, own_ref, keep_ref, give_ref, place_ref):
    owners, deep, _ = own_ref.shape
    block = own_ref[...]
    rows = block_rows(block, cap)
    slots, width = rows.shape
    ids = block[:, deep - NOTE :, :].astype(F32)[:, 0, :]
    side = jnp.where(ids >= owners, 1.0, 0.0)
    here = where_ref[3].astype(F32)
    upper = lax.broadcasted_iota(jnp.int32, (128, 128), 0) < lax.broadcasted_iota(
        jnp.int32, (128, 128), 1
    )
    lower = lax.broadcasted_iota(jnp.int32, (owners, owners), 1) < lax.broadcasted_iota(
        jnp.int32, (owners, owners), 0
    )
    upper = jnp.where(upper, 1.0, 0.0).astype(BF16)
    lower = jnp.where(lower, 1.0, 0.0).astype(BF16)
    sub = lax.broadcasted_iota(jnp.int32, (owners, cap, 128), 1)
    lane = lax.broadcasted_iota(jnp.int32, (owners, cap, 128), 2)
    ones = jnp.full((8, 128), 1.0, BF16)
    list_row = lax.broadcasted_iota(jnp.int32, (room, slots), 0).astype(F32)

    def as_row(grid):
        wide = jnp.broadcast_to(grid.reshape(owners, 1, 128), (owners, cap, 128))
        spread = jnp.where(sub == lane, wide, 0.0).reshape(slots, 128)
        return dot_t(ones, spread.astype(BF16))[0:1, :]

    members = []
    for part, out_ref in enumerate((keep_ref, give_ref)):
        chosen = (ids >= 0) & ((side == here) if part == 0 else (side != here))
        mask = jnp.where(chosen, 1.0, 0.0)
        packed = mask.astype(BF16)
        within = jnp.dot(packed, upper, preferred_element_type=F32)
        above = jnp.sum(jnp.dot(lower, packed, preferred_element_type=F32), axis=1, keepdims=True)
        after = jnp.where(chosen, within + above + 1.0, 0.0)
        high = jnp.floor(after * (1.0 / 32.0))
        rank = 32.0 * as_row(high) + as_row(after - 32.0 * high) - 1.0
        pick = jnp.where(list_row == rank, 1.0, 0.0).astype(BF16)
        out_ref[:room, :] = jnp.dot(pick, rows, preferred_element_type=F32).astype(BF16)
        place_ref[part * owners : (part + 1) * owners, :] = after - 1.0
        members.append(jnp.sum(jnp.sum(mask, axis=1, keepdims=True), axis=0, keepdims=True))
    over = jnp.where((members[0] > room) | (members[1] > room), 1.0, 0.0)
    spot = lax.broadcasted_iota(jnp.int32, (INFO, width), 1)
    for count, out_ref in zip(members, (keep_ref, give_ref)):
        high = jnp.floor(count * (1.0 / 32.0))
        info = jnp.where(spot == 0, high, jnp.where(spot == 1, count - 32.0 * high, over))
        out_ref[room:, :] = info.astype(BF16)


def split(where, own, cap, room):
    owners, deep, _ = own.shape
    width = (deep - NOTE) // cap * 128
    rows = owners * cap
    vmem = pl.BlockSpec(memory_space=pltpu.VMEM)
    return pl.pallas_call(
        functools.partial(split_kernel, cap, room),
        in_specs=[pl.BlockSpec(memory_space=pltpu.SMEM), vmem],
        out_shape=(
            jax.ShapeDtypeStruct((room + INFO, width), BF16),
            jax.ShapeDtypeStruct((room + INFO, width), BF16),
            jax.ShapeDtypeStruct((2 * owners, 128), F32),
        ),
        compiler_params=params(),
        cost_estimate=cost(4 * rows * room * width, 3 * rows * width),
    )(where, own)


def list_kernel(room, *refs):
    list_refs, out_ref = refs[:4], refs[4]
    over = jnp.zeros((1, 1), F32)
    counts = []
    for ref in list_refs:
        info = ref[room:, :128].astype(F32)
        counts.append(32.0 * info[0:1, 0:1] + info[0:1, 1:2])
        over = jnp.maximum(over, info[0:1, 2:3])
    other = lax.broadcasted_iota(jnp.int32, (room, room), 0)
    mine = lax.broadcasted_iota(jnp.int32, (room, room), 1)
    position = lax.broadcasted_iota(jnp.int32, (room, 1), 0).astype(F32)
    own = list_refs[0][:room, :]
    best = jnp.full((1, room), -1.0, F32)
    for j, ref in enumerate(list_refs):
        scores = dot_t(ref[:room, :], own)
        use = position < counts[j]
        if j == 0:
            use = use & (other != mine)
        best = jnp.maximum(best, jnp.max(jnp.where(use, scores, -1.0), axis=0, keepdims=True))
    out_ref[:, :room] = best
    out_ref[:, room:] = jnp.broadcast_to(over, (1, 128))


def list_best(lists, room):
    width = lists[0].shape[1]
    return pl.pallas_call(
        functools.partial(list_kernel, room),
        out_shape=jax.ShapeDtypeStruct((1, room + 128), F32),
        compiler_params=params(),
        cost_estimate=cost(8 * room * room * width, 8 * room * width),
    )(*lists)


def merge_kernel(owners, cap, room, kept_ref, back_ref, place_ref, mine_ref, other_ref, out_ref):
    slots = owners * cap
    sub = lax.broadcasted_iota(jnp.int32, (owners, cap, 128), 1)
    lane = lax.broadcasted_iota(jnp.int32, (owners, cap, 128), 2)
    spot = lax.broadcasted_iota(jnp.int32, (slots, room), 1).astype(F32)
    total = jnp.zeros((slots, 1), F32)
    for part, ref in enumerate((kept_ref, back_ref)):
        grid = place_ref[part * owners : (part + 1) * owners, :]
        wide = jnp.broadcast_to(grid.reshape(owners, 1, 128), (owners, cap, 128))
        spread = jnp.where(sub == lane, wide, 0.0).reshape(slots, 128)
        place = jnp.sum(spread, axis=1, keepdims=True)
        found = jnp.where(spot == place, ref[:, :room], 0.0)
        total = total + jnp.sum(found, axis=1, keepdims=True)
    out_ref[:, :cap] = column_to_grid(total, owners, cap)
    out_ref[:, cap : 2 * cap] = jnp.maximum(mine_ref[...], other_ref[...])
    out_ref[:, 2 * cap :] = jnp.broadcast_to(kept_ref[:, room : room + cap], (owners, cap))


def merge(kept, back, place, mine, other, room):
    owners, cap = mine.shape
    return pl.pallas_call(
        functools.partial(merge_kernel, owners, cap, room),
        out_shape=jax.ShapeDtypeStruct((owners, 3 * cap), F32),
        compiler_params=params(),
    )(kept, back, place, mine, other)


def unpack_kernel(owners, cap, back_ref, place_ref, dup_ref, *more_refs):
    back = back_ref[...]
    target = place_ref[0:1, :]
    rank = place_ref[1:2, :]
    rows = target.shape[1]
    found = jnp.full((owners, rows), -2.0, F32)
    for k in range(cap):
        found = jnp.where(rank == k, back[:, k : k + 1], found)
    owner_of = lax.broadcasted_iota(jnp.int32, (owners, rows), 0)
    dup_ref[...] = jnp.max(jnp.where(target == owner_of, found, -2.0), axis=0, keepdims=True)
    for k, ref in enumerate(more_refs):
        ref[...] = jnp.max(back[:, (k + 1) * cap : (k + 2) * cap], axis=0, keepdims=True)


def unpack(back, place, owners, cap):
    rows = place.shape[1]
    more = back.shape[1] // cap - 1
    return pl.pallas_call(
        functools.partial(unpack_kernel, owners, cap),
        out_shape=[jax.ShapeDtypeStruct((1, rows), F32)]
        + [jax.ShapeDtypeStruct((1, cap), F32)] * more,
        compiler_params=params(),
    )(back, place)


def join_kernel(*refs):
    out_ref, at = refs[-1], 0
    for ref in refs[:-1]:
        out_ref[at : at + ref.shape[0], :] = ref[...]
        at += ref.shape[0]


def join(*blocks):
    rows, width = sum(b.shape[0] for b in blocks), blocks[0].shape[1]
    return pl.pallas_call(
        join_kernel,
        out_shape=jax.ShapeDtypeStruct((rows, width), blocks[0].dtype),
        compiler_params=params(),
        cost_estimate=cost(0, 4 * rows * width),
    )(*blocks)


def full_scores(own, place, cap):
    owners = own.shape[0]
    own_x = lax.ppermute(own, "xl", SWAP)
    own_c = lax.ppermute(own, "c", SWAP)
    own_cx = lax.ppermute(own_x, "c", SWAP)
    held = dup_best(own, [own, own_c], cap, with_self=True)
    best = dup_best(own, [own_x, own_cx], cap, old=held, last=True)
    back = lax.all_to_all(best, OWN, split_axis=0, concat_axis=0, tiled=True)
    return unpack(back, place, owners, cap)[0]


def moved(block, axis, size, by):
    return lax.ppermute(block, axis, [(i, (i - by) % size) for i in range(size)])


def shards(embeddings, cluster_of, new_rows, centroids):
    owners = lax.axis_size(OWN)
    rows, width = embeddings.shape
    cap = 2 * rows // owners
    room = 3 * rows // 4
    where = jnp.stack([lax.axis_index(a) for a in (*OWN, "xl")]).astype(jnp.int32)

    cents = lax.all_gather(unit(centroids), ("xh", "xl"), axis=0, tiled=True)
    line = join(new_rows, *(moved(new_rows, "z", 8, k) for k in (2, 4, 6)))
    steps_z = (0, 2, 4, 6, 1, 3, 5, 7)
    send, place = pack(embeddings, cluster_of, owners, cap)
    landed = lax.all_to_all(send, OWN, split_axis=0, concat_axis=0, tiled=True)
    own = tie(landed, cents, line)

    keep, give, spots = split(where, own, cap, room)
    came = lax.ppermute(give, "xl", SWAP)
    keep_c = lax.ppermute(keep, "c", SWAP)

    steps_y = (0, -1, 1, -2)
    line = join(line, moved(line, "z", 8, 1))
    left = lax.ppermute(line, "y", [(i, (i + 1) % 4) for i in range(4)])
    right = lax.ppermute(line, "y", [(i, (i + 3) % 4) for i in range(4)])
    far = lax.ppermute(line, "y", [(i, (i + 2) % 4) for i in range(4)])
    new = join(line, left, right, far)
    new_other = lax.ppermute(new, "c", SWAP)
    cent_mine, cent_theirs = cent_best(
        where, new, new_other, cents, owners, new_rows.shape[0], steps_y, steps_z
    )
    cent_back = lax.ppermute(cent_theirs, "c", SWAP)

    came_c = lax.ppermute(came, "c", SWAP)
    guests = lax.ppermute(list_best([came, keep, keep_c, came_c], room), "xl", SWAP)
    kept = list_best([keep, came, keep_c, came_c], room)
    both = merge(kept, guests, spots, cent_mine, cent_back, room)
    back = lax.all_to_all(both, OWN, split_axis=0, concat_axis=0, tiled=True)
    dup, cent_score, over = unpack(back, place, owners, cap)
    dup = lax.cond(
        over[0, 0] > 0.5,
        lambda held, spot, short: full_scores(held, spot, cap),
        lambda held, spot, short: short,
        own,
        place,
        dup,
    )
    return (dup.reshape(rows), cent_score.reshape(new_rows.shape[0]))


def solution(mesh):
    sizes = mesh.devices.shape
    owners, group = sizes
    halves = owners // 2
    inner = Mesh(mesh.devices.reshape(halves // 4, 4, 2, group // 2, 2), ALL)
    return jax.shard_map(
        shards,
        mesh=inner,
        in_specs=(P(ALL, None), P(ALL), P(ALL, None), P(ALL, None)),
        out_specs=(P(ALL), P(ALL)),
        check_vma=False,
    )
```
